32 devices in a mesh: sub: 8 (over z, x), row: 4 (over y, core).
Axes of the slice: x: 2, y: 2, z: 4, core: 2. Of those that a mesh axis runs over, the one named last changes fastest.
Arguments:
- residual: float32 [32, 8, 2048], P(None, 'sub', 'row')
- factor: float32 [8, 3072, 3072], P('sub', 'row'), may hold values from -0.0390625 to 0.0390625
- basis: float32 [96, 8, 2048], P(None, 'sub', 'row'), may hold values from -0.046875 to 0.046875
- send_rows: int32 [8, 2, 512], P('sub'), may hold values from 0 to 2047, as said below
Outputs:
- coeffs: float32 [96, 32], replicated
- rfactor: float32 [32, 32], replicated
- block_q: float32 [32, 8, 2048], P(None, 'sub', 'row')
The draws below stay inside these ranges and needn't reach their ends.
Inputs may be any that keep to these rules, and one draw needn't show every extreme that they name: Within each send_rows[s, side, :] the rows are distinct.
All inputs are finite; a program needn't handle non-finite values.
Results may differ from the reference program's by a relative error of at most 0.000073.
Values sent between devices are 32-bit elements; how exact they have to be, the bound alone decides.
A program may use at most 64 MiB of HBM per device.

```python
import math
import jax
import jax.numpy as jnp
from jax import lax

VECS = 32
BASIS = 96
OV = 512
SUBS = 8
SUB_ROWS = 2048
EXT = 3072
ROWS = 16384


def draw_residual(key, part):
    key_noise, key_cell = jax.random.split(key, 2)
    position = jnp.arange(SUBS, dtype=jnp.float32) / (SUBS - 1)
    trend = (1.0 + 2.0 * position)[None, :, None]
    cell = jnp.exp(math.log(10.0) * jax.random.uniform(key_cell, (1, SUBS, SUB_ROWS), jnp.float32))
    noise = jax.random.normal(key_noise, (VECS, SUBS, SUB_ROWS), jnp.float32)
    values = noise * cell * trend * 0.1
    return values.astype(jnp.float32)


def draw_send_rows(key, part):
    keys = jax.random.split(jax.random.fold_in(key, 7), SUBS * 2)
    picked = jax.vmap(lambda one_key: jax.random.permutation(one_key, SUB_ROWS)[:OV])(keys)
    return picked.reshape(SUBS, 2, OV).astype(jnp.int32)


def steps_of(key, extent, shards, smallest, top_value):
    gain = 1.0
    for dim, parts in shards:
        draws = jax.random.uniform(jax.random.fold_in(jax.random.fold_in(key, 6), dim), (parts,), jnp.float32, smallest / len(shards), top_value / len(shards))
        gain = gain * jnp.repeat(jnp.exp(draws), extent[dim] // parts).reshape((-1,) + (1,) * (len(extent) - 1 - dim))
    return gain


def normal_values(key, extent, deviation, limit, pieces=(), kind=jnp.bfloat16):
    drawn = deviation * jax.random.normal(key, extent, jnp.float32)
    if pieces:
        drawn = drawn * steps_of(key, extent, pieces, -0.22, 0.18)
    return jnp.clip(drawn, -limit, limit).astype(kind)


def setup_inputs(seed: int = 0) -> dict:
    key_of = jax.random.split(jax.random.key(seed), 5)
    residual = draw_residual(jax.random.fold_in(key_of[4], 71), 0)
    factor = normal_values(key_of[1], (SUBS, EXT, EXT), (8 * EXT) ** -0.5, 0.0390625, ((0, 8), (1, 4)), jnp.float32)
    basis = normal_values(key_of[2], (BASIS, SUBS, SUB_ROWS), ROWS ** -0.5, 0.046875, ((1, 8), (2, 4)), jnp.float32)
    send_rows = draw_send_rows(jax.random.fold_in(key_of[4], 71), 0)
    return {"residual": residual, "factor": factor, "basis": basis, "send_rows": send_rows}


HIGH = lax.Precision.HIGHEST

def apply_block(pair):
    extended, factor_block = pair
    size = factor_block.shape[0]
    full = factor_block + jnp.eye(size, dtype=factor_block.dtype)
    inner = lax.dot_general(extended, full, (((1,), (1,)), ((), ())), precision=HIGH)
    return jnp.dot(inner, full, precision=HIGH)

def pick_rows(block, rows_index):
    return block[:, rows_index]

def add_rows(block, values, rows_index):
    return block.at[:, rows_index].add(values)

def reference(residual, factor, basis, send_rows):
    zero_rim = jnp.zeros((VECS, 1, OV), residual.dtype)
    to_lower = jax.vmap(pick_rows, in_axes=(1, 0), out_axes=1)(residual, send_rows[:, 0])
    to_upper = jax.vmap(pick_rows, in_axes=(1, 0), out_axes=1)(residual, send_rows[:, 1])
    from_lower = jnp.concatenate([zero_rim, to_upper[:, :-1]], axis=1)
    from_upper = jnp.concatenate([to_lower[:, 1:], zero_rim], axis=1)
    extended = jnp.concatenate([residual, from_lower, from_upper], axis=2)
    local = lax.map(apply_block, (jnp.transpose(extended, (1, 0, 2)), factor))
    own_part = local[:, :, :SUB_ROWS]
    lower_part = local[:, :, SUB_ROWS:SUB_ROWS + OV]
    upper_part = local[:, :, SUB_ROWS + OV:]
    zero_back = jnp.zeros((1, VECS, OV), residual.dtype)
    back_from_upper = jnp.concatenate([lower_part[1:], zero_back], axis=0)
    back_from_lower = jnp.concatenate([zero_back, upper_part[:-1]], axis=0)
    summed = jax.vmap(add_rows)(own_part, back_from_upper, send_rows[:, 1])
    summed = jax.vmap(add_rows)(summed, back_from_lower, send_rows[:, 0])
    block_t = jnp.transpose(summed, (1, 0, 2)).reshape(VECS, ROWS)
    vectors = basis.reshape(BASIS, ROWS)
    first = lax.dot_general(vectors, block_t, (((1,), (1,)), ((), ())), precision=HIGH)
    once = block_t - lax.dot_general(first, vectors, (((0,), (0,)), ((), ())), precision=HIGH)
    second = lax.dot_general(vectors, once, (((1,), (1,)), ((), ())), precision=HIGH)
    twice = once - lax.dot_general(second, vectors, (((0,), (0,)), ((), ())), precision=HIGH)
    gram = lax.dot_general(twice, twice, (((1,), (1,)), ((), ())), precision=HIGH) / ROWS
    lower_tri = jnp.linalg.cholesky(gram)
    solved = jax.scipy.linalg.solve_triangular(lower_tri, twice, lower=True)
    return (first + second, lower_tri.T, solved.reshape(VECS, SUBS, SUB_ROWS))
```

```python
import functools

import jax
import jax.numpy as jnp
from jax import lax
from jax.experimental import pallas as pl
from jax.experimental.pallas import tpu as pltpu
from jax.sharding import PartitionSpec as P

HIGH = lax.Precision.HIGHEST
MESH = pl.DeviceIdType.MESH
F32 = jnp.float32
BF16 = jnp.bfloat16
LOADS = 6


def dot_nt(left, right, precision=None):
    return lax.dot_general(
        left, right, (((1,), (1,)), ((), ())), precision=precision, preferred_element_type=F32
    )


def dot_nn(left, right, precision=None):
    return lax.dot_general(
        left, right, (((1,), (0,)), ((), ())), precision=precision, preferred_element_type=F32
    )


def split_two(value):
    high = value.astype(BF16)
    return high, (value - high.astype(F32)).astype(BF16)


def split_three(value):
    high = value.astype(BF16)
    rest = value - high.astype(F32)
    mid = rest.astype(BF16)
    return high, mid, (rest - mid.astype(F32)).astype(BF16)


def factor_gram(gram, vecs):
    eye = (
        lax.broadcasted_iota(jnp.int32, (vecs, vecs), 0)
        == lax.broadcasted_iota(jnp.int32, (vecs, vecs), 1)
    ).astype(F32)
    work = jnp.concatenate([gram, eye, jnp.zeros((vecs, 128 - 2 * vecs), F32)], axis=1)
    row_of = lax.broadcasted_iota(jnp.int32, (vecs, 1), 0)
    for step in range(vecs - 1):
        scale = 1.0 / work[step : step + 1, step : step + 1]
        multiplier = jnp.where(row_of > step, work[:, step : step + 1] * scale, 0.0)
        work = work - multiplier * work[step : step + 1, :]
    rows = lax.broadcasted_iota(jnp.int32, work.shape, 0)
    lanes = lax.broadcasted_iota(jnp.int32, work.shape, 1)
    pivots = jnp.sum(jnp.where(rows == lanes, work, 0.0), axis=1, keepdims=True)
    work = jnp.where(lanes >= rows, work, 0.0) * (1.0 / jnp.sqrt(pivots))
    return work[:, :vecs], work[:, vecs : 2 * vecs]


def kernel(
    subs,
    rows_n,
    res_ref,
    fac_ref,
    bas_ref,
    idx_ref,
    coef_ref,
    rfac_ref,
    q_ref,
    fac,
    fhi,
    flo,
    ext,
    stack,
    sel,
    acc,
    part,
    rs_own,
    rs_mar,
    back_q,
    back,
    hot,
    vpad,
    g_part,
    g_rs,
    g_sub,
    g_full,
    f_row,
    f_sub,
    c_row,
    c_sub,
    load_sem,
    row_send,
    row_recv,
    near_send,
    near_recv,
    sub_send,
    sub_recv,
):
    sub = lax.axis_index("sub")
    row = lax.axis_index("row")
    vecs, slab = res_ref.shape
    share, wide = fac_ref.shape
    nb = bas_ref.shape[0]
    margin = idx_ref.shape[1]
    own = slab * rows_n
    quarter = margin // rows_n
    total_rows = own * subs
    has_lower = sub > 0
    has_upper = sub < subs - 1
    started = []

    def row_peer(k):
        return lax.rem(row + k, rows_n)

    def sub_peer(k):
        return lax.rem(sub + k, subs)

    load_rows = share // LOADS
    loads = []
    for i in range(LOADS):
        span = pl.ds(i * load_rows, load_rows)
        loads.append(pltpu.make_async_copy(fac_ref.at[span], fac.at[span], load_sem.at[i]))
        loads[-1].start()

    barrier = pltpu.get_barrier_semaphore()

    def greet(to_sub, to_row):
        pl.semaphore_signal(barrier, inc=1, device_id=(to_sub, to_row), device_id_type=MESH)

    for k in range(1, rows_n):
        greet(sub, row_peer(k))

    @pl.when(has_lower)
    def _():
        for k in range(1, rows_n):
            greet(sub - 1, row_peer(k))

    @pl.when(has_upper)
    def _():
        for k in range(1, rows_n):
            greet(sub + 1, row_peer(k))

    for k in range(1, subs):
        greet(sub_peer(k), row)
    near = has_lower.astype(jnp.int32) + has_upper.astype(jnp.int32)
    ext[:, pl.ds(pl.multiple_of(row * slab, 128), slab)] = res_ref[...]
    pl.semaphore_wait(barrier, (rows_n - 1) * (1 + near) + subs - 1)

    def row_copies(slot, source_of, target_of):
        copies = []
        for k in range(1, rows_n):
            peer = row_peer(k)
            copies.append(
                pltpu.make_async_remote_copy(
                    source_of(peer),
                    target_of(k),
                    row_send.at[slot, k - 1],
                    row_recv.at[slot, k - 1],
                    device_id=(sub, peer),
                    device_id_type=MESH,
                )
            )
            copies[-1].start()
        started.extend(copies)
        return copies

    def sub_copies(slot, ref):
        copies = []
        for k in range(1, subs):
            copies.append(
                pltpu.make_async_remote_copy(
                    ref.at[sub],
                    ref.at[sub],
                    sub_send.at[slot, k - 1],
                    sub_recv.at[slot, k - 1],
                    device_id=(sub_peer(k), row),
                    device_id_type=MESH,
                )
            )
            copies[-1].start()
        started.extend(copies)
        return copies

    def near_copies(slot, up, source, target):
        to_sub = sub + 1 if up else sub - 1
        return [
            pltpu.make_async_remote_copy(
                source,
                target,
                near_send.at[slot, k],
                near_recv.at[slot, k],
                device_id=(to_sub, row_peer(k)),
                device_id_type=MESH,
            )
            for k in range(rows_n)
        ]

    def near_start(up, copies):
        @pl.when(has_upper if up else has_lower)
        def _():
            for copy in copies:
                copy.start()

    def near_wait(up, copies):
        @pl.when(has_lower if up else has_upper)
        def _():
            for copy in copies:
                copy.wait_recv()

    def near_finish(up, copies):
        @pl.when(has_upper if up else has_lower)
        def _():
            for copy in copies:
                copy.wait_send()

    def landed(copies):
        for copy in copies:
            copy.wait_recv()

    slab_copies = row_copies(
        0,
        lambda peer: res_ref,
        lambda k: ext.at[:, pl.ds(pl.multiple_of(row * slab, 128), slab)],
    )

    vpad[:nb] = bas_ref[...]
    vpad[nb:] = jnp.zeros((vpad.shape[0] - nb, slab), F32)
    g_part[...] = dot_nt(vpad[...], vpad[...], HIGH)
    g_rows = nb // rows_n

    def g_span(which):
        return pl.ds(pl.multiple_of(which * g_rows, 8), g_rows)

    g_copies = row_copies(1, lambda peer: g_part.at[g_span(peer)], lambda k: g_rs.at[k - 1])

    for i in range(LOADS):
        loads[i].wait()

        @pl.loop(0, load_rows // 16)
        def _(j):
            span = pl.ds(pl.multiple_of(i * load_rows + j * 16, 16), 16)
            high, low = split_two(fac[span, :])
            fhi[span, :] = high
            flo[span, :] = low

    base = lax.broadcasted_iota(jnp.int32, (own, quarter), 0)
    picks = []
    for side in range(2):
        index = idx_ref[side : side + 1, pl.ds(pl.multiple_of(row * quarter, 128), quarter)]
        picks.append((base == index).astype(F32).astype(BF16))
    pick = jnp.concatenate(picks, axis=1)
    landed(slab_copies)
    whole = ext[:, :own]
    pieces = jnp.concatenate(split_three(whole), axis=0)
    chosen = dot_nn(pieces, pick)
    chosen = chosen[:vecs] + chosen[vecs : 2 * vecs] + chosen[2 * vecs :]
    sel[0] = chosen[:, :quarter]
    sel[1] = chosen[:, quarter:]

    def ext_span(side):
        return ext.at[:, pl.ds(pl.multiple_of(own + side * margin + row * quarter, 128), quarter)]

    up_copies = near_copies(0, True, sel.at[1], ext_span(0))
    down_copies = near_copies(1, False, sel.at[0], ext_span(1))
    near_start(True, up_copies)
    near_start(False, down_copies)

    @pl.when(jnp.logical_not(has_lower))
    def _():
        ext[:, own : own + margin] = jnp.zeros((vecs, margin), F32)

    @pl.when(jnp.logical_not(has_upper))
    def _():
        ext[:, own + margin :] = jnp.zeros((vecs, margin), F32)

    landed(g_copies)
    g_mine = g_part[g_span(row), :]
    for k in range(1, rows_n):
        g_mine = g_mine + g_rs[k - 1]
    g_sub[sub] = g_mine
    g_across = sub_copies(0, g_sub)

    high, low = split_two(whole)
    stack[:vecs, :own] = high
    stack[vecs:, :own] = low
    step = 256

    def first_product(lo, hi, add):
        for j in range(0, share, step):
            both = dot_nt(stack[:, lo:hi], fhi[j : j + step, lo:hi])
            value = both[:vecs] + both[vecs:] + dot_nt(stack[:vecs, lo:hi], flo[j : j + step, lo:hi])
            acc[:, j : j + step] = acc[:, j : j + step] + value if add else value

    first_product(0, own, False)
    my_rows = row * slab + lax.broadcasted_iota(jnp.int32, (slab, margin), 0)
    hot[:, :margin] = (my_rows == idx_ref[1:2, :]).astype(F32).astype(BF16)
    hot[:, margin:] = (my_rows == idx_ref[0:1, :]).astype(F32).astype(BF16)
    near_wait(True, up_copies)
    near_wait(False, down_copies)
    high, low = split_two(ext[:, own:])
    stack[:vecs, own:] = high
    stack[vecs:, own:] = low
    first_product(own, wide, True)
    mine_cols = pl.ds(pl.multiple_of(row * share, 128), share)
    inner = acc[...] + ext[:, mine_cols]
    part[...] = jnp.zeros((vecs, wide), F32)
    part[:, mine_cols] = inner

    landed(g_across)
    g_sum = g_sub[0]
    for k in range(1, subs):
        g_sum = g_sum + g_sub[k]
    g_full[g_span(row), :] = g_sum
    g_full[nb:, :] = jnp.zeros((g_full.shape[0] - nb, g_full.shape[1]), F32)
    g_gather = row_copies(
        2, lambda peer: g_full.at[g_span(row)], lambda k: g_full.at[g_span(row)]
    )

    high, low = split_two(inner)
    both_in = jnp.concatenate([high, low], axis=0)

    def second_product(lo):
        both = dot_nn(both_in, fhi[:, lo : lo + slab])
        value = both[:vecs] + both[vecs:] + dot_nn(high, flo[:, lo : lo + slab])
        part[:, lo : lo + slab] = part[:, lo : lo + slab] + value

    for lo in range(own, wide, slab):
        second_product(lo)

    def margin_of(side, which):
        return part.at[:, pl.ds(pl.multiple_of(own + side * margin + which * quarter, 128), quarter)]

    mar0 = row_copies(3, lambda peer: margin_of(0, peer), lambda k: rs_mar.at[k - 1, 0])
    mar1 = row_copies(4, lambda peer: margin_of(1, peer), lambda k: rs_mar.at[k - 1, 1])
    for lo in range(0, own, slab):
        second_product(lo)

    def own_of(which):
        return part.at[:, pl.ds(pl.multiple_of(which * slab, 128), slab)]

    own_copies = row_copies(5, own_of, lambda k: rs_own.at[k - 1])
    landed(mar0)
    landed(mar1)
    for side in range(2):
        total = margin_of(side, row)[...]
        for k in range(1, rows_n):
            total = total + rs_mar[k - 1, side]
        back_q[side] = total

    def back_span(side):
        return back.at[:, pl.ds(pl.multiple_of(side * margin + row * quarter, 128), quarter)]

    back_down = near_copies(2, False, back_q.at[0], back_span(0))
    back_up = near_copies(3, True, back_q.at[1], back_span(1))
    near_start(False, back_down)
    near_start(True, back_up)

    @pl.when(jnp.logical_not(has_upper))
    def _():
        back[:, :margin] = jnp.zeros((vecs, margin), F32)

    @pl.when(jnp.logical_not(has_lower))
    def _():
        back[:, margin:] = jnp.zeros((vecs, margin), F32)

    landed(own_copies)
    block_t = own_of(row)[...]
    for k in range(1, rows_n):
        block_t = block_t + rs_own[k - 1]
    landed(g_gather)
    near_wait(False, back_down)
    near_wait(True, back_up)
    added = dot_nt(jnp.concatenate(split_three(back[...]), axis=0), hot[...])
    block_t = block_t + (added[:vecs] + added[vecs : 2 * vecs] + added[2 * vecs :])

    def sum_all(value, slot, row_slot, by_row, by_sub):
        by_row[row] = value
        landed(row_copies(row_slot, lambda peer: by_row.at[row], lambda k: by_row.at[row]))
        total = by_row[0]
        for k in range(1, rows_n):
            total = total + by_row[k]
        by_sub[sub] = total
        landed(sub_copies(slot, by_sub))
        total = by_sub[0]
        for k in range(1, subs):
            total = total + by_sub[k]
        return total

    first = sum_all(dot_nt(block_t, vpad[...], HIGH), 1, 6, f_row, f_sub)
    second = first - dot_nn(first, g_full[...], HIGH)
    coeffs = first + second
    twice = block_t - dot_nn(coeffs, vpad[...], HIGH)
    gram = dot_nt(twice, twice, HIGH)
    fold = 128 // vecs
    tall = vecs // fold
    packed = jnp.concatenate([gram[i * tall : (i + 1) * tall] for i in range(fold)], axis=1)
    coef_ref[...] = coeffs.T[:nb]
    packed = sum_all(packed, 2, 7, c_row, c_sub) * (1.0 / total_rows)
    gram = jnp.concatenate([packed[:, i * vecs : (i + 1) * vecs] for i in range(fold)], axis=0)
    upper, inverse = factor_gram(gram, vecs)
    rfac_ref[...] = upper
    q_ref[...] = dot_nn(inverse, twice, HIGH)

    for copy in started:
        copy.wait_send()
    near_finish(True, up_copies)
    near_finish(False, down_copies)
    near_finish(False, back_down)
    near_finish(True, back_up)


def per_device(residual, factor, basis, send_rows):
    subs = lax.axis_size("sub")
    rows_n = lax.axis_size("row")
    vecs, _, slab = residual.shape
    nb = basis.shape[0]
    _, share, wide = factor.shape
    margin = send_rows.shape[2]
    quarter = margin // rows_n
    pad = -(-nb // 128) * 128
    g_rows = nb // rows_n
    fold = 128 // vecs
    vmem = pl.BlockSpec(memory_space=pltpu.VMEM)
    coeffs, rfactor, block_q = pl.pallas_call(
        functools.partial(kernel, subs, rows_n),
        out_shape=(
            jax.ShapeDtypeStruct((nb, vecs), F32),
            jax.ShapeDtypeStruct((vecs, vecs), F32),
            jax.ShapeDtypeStruct((vecs, slab), F32),
        ),
        in_specs=[vmem, pl.BlockSpec(memory_space=pl.ANY), vmem, vmem],
        out_specs=(vmem, vmem, vmem),
        scratch_shapes=[
            pltpu.VMEM((share, wide), F32),
            pltpu.VMEM((share, wide), BF16),
            pltpu.VMEM((share, wide), BF16),
            pltpu.VMEM((vecs, wide), F32),
            pltpu.VMEM((2 * vecs, wide), BF16),
            pltpu.VMEM((2, vecs, quarter), F32),
            pltpu.VMEM((vecs, share), F32),
            pltpu.VMEM((vecs, wide), F32),
            pltpu.VMEM((rows_n - 1, vecs, slab), F32),
            pltpu.VMEM((rows_n - 1, 2, vecs, quarter), F32),
            pltpu.VMEM((2, vecs, quarter), F32),
            pltpu.VMEM((vecs, 2 * margin), F32),
            pltpu.VMEM((slab, 2 * margin), BF16),
            pltpu.VMEM((pad, slab), F32),
            pltpu.VMEM((pad, pad), F32),
            pltpu.VMEM((rows_n - 1, g_rows, pad), F32),
            pltpu.VMEM((subs, g_rows, pad), F32),
            pltpu.VMEM((pad, pad), F32),
            pltpu.VMEM((rows_n, vecs, pad), F32),
            pltpu.VMEM((subs, vecs, pad), F32),
            pltpu.VMEM((rows_n, vecs // fold, 128), F32),
            pltpu.VMEM((subs, vecs // fold, 128), F32),
            pltpu.SemaphoreType.DMA((LOADS,)),
            pltpu.SemaphoreType.DMA((8, rows_n - 1)),
            pltpu.SemaphoreType.DMA((8, rows_n - 1)),
            pltpu.SemaphoreType.DMA((4, rows_n)),
            pltpu.SemaphoreType.DMA((4, rows_n)),
            pltpu.SemaphoreType.DMA((3, subs - 1)),
            pltpu.SemaphoreType.DMA((3, subs - 1)),
        ],
        compiler_params=pltpu.CompilerParams(
            collective_id=0, has_side_effects=True, vmem_limit_bytes=40 * 1024 * 1024
        ),
        cost_estimate=pl.CostEstimate(
            flops=12 * vecs * share * wide, bytes_accessed=4 * share * wide, transcendentals=0
        ),
    )(residual[:, 0, :], factor[0], basis[:, 0, :], send_rows[0])
    return coeffs, rfactor, block_q[:, None, :]


def solution(mesh):
    placed = (
        P(None, "sub", "row"),
        P("sub", "row", None),
        P(None, "sub", "row"),
        P("sub", None, None),
    )
    return jax.shard_map(
        per_device,
        mesh=mesh,
        in_specs=placed,
        out_specs=(P(), P(), P(None, "sub", "row")),
        check_vma=False,
    )
```

```python
import functools

import jax
import jax.numpy as jnp
from jax import lax
from jax.experimental import pallas as pl
from jax.experimental.pallas import tpu as pltpu
from jax.sharding import PartitionSpec as P

HIGH = lax.Precision.HIGHEST
MESH = pl.DeviceIdType.MESH
F32 = jnp.float32
BF16 = jnp.bfloat16
LOADS = 6


def dot_nt(left, right, precision=None):
    return lax.dot_general(
        left, right, (((1,), (1,)), ((), ())), precision=precision, preferred_element_type=F32
    )


def dot_nn(left, right, precision=None):
    return lax.dot_general(
        left, right, (((1,), (0,)), ((), ())), precision=precision, preferred_element_type=F32
    )


def split_two(value):
    high = value.astype(BF16)
    return high, (value - high.astype(F32)).astype(BF16)


def split_three(value):
    high = value.astype(BF16)
    rest = value - high.astype(F32)
    mid = rest.astype(BF16)
    return high, mid, (rest - mid.astype(F32)).astype(BF16)


def factor_gram(gram, vecs):
    eye = (
        lax.broadcasted_iota(jnp.int32, (vecs, vecs), 0)
        == lax.broadcasted_iota(jnp.int32, (vecs, vecs), 1)
    ).astype(F32)
    work = jnp.concatenate([gram, eye, jnp.zeros((vecs, 128 - 2 * vecs), F32)], axis=1)
    row_of = lax.broadcasted_iota(jnp.int32, (vecs, 1), 0)
    for step in range(vecs - 1):
        scale = 1.0 / work[step : step + 1, step : step + 1]
        multiplier = jnp.where(row_of > step, work[:, step : step + 1] * scale, 0.0)
        work = work - multiplier * work[step : step + 1, :]
    rows = lax.broadcasted_iota(jnp.int32, work.shape, 0)
    lanes = lax.broadcasted_iota(jnp.int32, work.shape, 1)
    pivots = jnp.sum(jnp.where(rows == lanes, work, 0.0), axis=1, keepdims=True)
    work = jnp.where(lanes >= rows, work, 0.0) * (1.0 / jnp.sqrt(pivots))
    return work[:, :vecs], work[:, vecs : 2 * vecs]


def kernel(
    subs,
    rows_n,
    res_hbm,
    fac_hbm,
    bas_hbm,
    idx_hbm,
    coef_ref,
    gram_ref,
    twice_ref,
    res_ref,
    bas_ref,
    idx_ref,
    fac,
    fhi,
    flo,
    ext,
    stack,
    sel,
    acc,
    part,
    rs_own,
    rs_mar,
    back_q,
    back,
    hot,
    vpad,
    g_part,
    g_rs,
    g_sub,
    g_full,
    f_row,
    f_sub,
    c_row,
    c_sub,
    f_part,
    c_full,
    small_sem,
    load_sem,
    row_send,
    row_recv,
    near_send,
    near_recv,
    sub_send,
    sub_recv,
):
    sub = lax.axis_index("sub")
    row = lax.axis_index("row")
    vecs, _, slab = res_ref.shape
    share, wide = fac.shape
    nb = bas_ref.shape[0]
    margin = idx_ref.shape[1]
    own = slab * rows_n
    quarter = margin // rows_n
    total_rows = own * subs
    has_lower = sub > 0
    has_upper = sub < subs - 1
    started = []

    def row_peer(k):
        return lax.rem(row + k, rows_n)

    def sub_peer(k):
        return lax.rem(sub + k, subs)

    small = [
        pltpu.make_async_copy(source, target, small_sem.at[i])
        for i, (source, target) in enumerate(
            [(res_hbm, res_ref), (idx_hbm.at[0], idx_ref), (bas_hbm, bas_ref)]
        )
    ]
    for copy in small:
        copy.start()
    load_rows = share // LOADS
    loads = []
    for i in range(LOADS):
        span = pl.ds(i * load_rows, load_rows)
        loads.append(pltpu.make_async_copy(fac_hbm.at[0, span], fac.at[span], load_sem.at[i]))
        loads[-1].start()

    barrier = pltpu.get_barrier_semaphore()

    def greet(to_sub, to_row):
        pl.semaphore_signal(barrier, inc=1, device_id=(to_sub, to_row), device_id_type=MESH)

    for k in range(1, rows_n):
        greet(sub, row_peer(k))

    @pl.when(has_lower)
    def _():
        for k in range(1, rows_n):
            greet(sub - 1, row_peer(k))

    @pl.when(has_upper)
    def _():
        for k in range(1, rows_n):
            greet(sub + 1, row_peer(k))

    for k in range(1, subs):
        greet(sub_peer(k), row)
    near = has_lower.astype(jnp.int32) + has_upper.astype(jnp.int32)
    own_slab = ext.at[:, pl.ds(pl.multiple_of(row * slab, 128), slab)]
    small[0].wait()
    own_slab[...] = res_ref[:, 0, :]
    pl.semaphore_wait(barrier, (rows_n - 1) * (1 + near) + subs - 1)

    def row_copies(slot, source_of, target_of):
        copies = []
        for k in range(1, rows_n):
            peer = row_peer(k)
            copies.append(
                pltpu.make_async_remote_copy(
                    source_of(peer),
                    target_of(k),
                    row_send.at[slot, k - 1],
                    row_recv.at[slot, k - 1],
                    device_id=(sub, peer),
                    device_id_type=MESH,
                )
            )
            copies[-1].start()
        started.extend(copies)
        return copies

    def sub_copies(slot, ref):
        copies = []
        for k in range(1, subs):
            copies.append(
                pltpu.make_async_remote_copy(
                    ref.at[sub],
                    ref.at[sub],
                    sub_send.at[slot, k - 1],
                    sub_recv.at[slot, k - 1],
                    device_id=(sub_peer(k), row),
                    device_id_type=MESH,
                )
            )
            copies[-1].start()
        started.extend(copies)
        return copies

    def near_copies(slot, up, source, target):
        to_sub = sub + 1 if up else sub - 1
        return [
            pltpu.make_async_remote_copy(
                source,
                target,
                near_send.at[slot, k],
                near_recv.at[slot, k],
                device_id=(to_sub, row_peer(k)),
                device_id_type=MESH,
            )
            for k in range(rows_n)
        ]

    def near_start(up, copies):
        @pl.when(has_upper if up else has_lower)
        def _():
            for copy in copies:
                copy.start()

    def near_wait(up, copies):
        @pl.when(has_lower if up else has_upper)
        def _():
            for copy in copies:
                copy.wait_recv()

    def near_finish(up, copies):
        @pl.when(has_upper if up else has_lower)
        def _():
            for copy in copies:
                copy.wait_send()

    def landed(copies):
        for copy in copies:
            copy.wait_recv()

    slab_copies = row_copies(0, lambda peer: own_slab, lambda k: own_slab)
    small[1].wait()
    base = lax.broadcasted_iota(jnp.int32, (own, quarter), 0)
    picks = []
    for side in range(2):
        index = idx_ref[side : side + 1, pl.ds(pl.multiple_of(row * quarter, 128), quarter)]
        picks.append((base == index).astype(F32).astype(BF16))
    pick = jnp.concatenate(picks, axis=1)
    small[2].wait()
    vpad[:nb] = bas_ref[:, 0, :]
    vpad[nb:] = jnp.zeros((vpad.shape[0] - nb, slab), F32)
    landed(slab_copies)
    whole = ext[:, :own]
    pieces = jnp.concatenate(split_three(whole), axis=0)
    chosen = dot_nn(pieces, pick)
    chosen = chosen[:vecs] + chosen[vecs : 2 * vecs] + chosen[2 * vecs :]
    sel[0] = chosen[:, :quarter]
    sel[1] = chosen[:, quarter:]

    def ext_span(side):
        return ext.at[:, pl.ds(pl.multiple_of(own + side * margin + row * quarter, 128), quarter)]

    up_copies = near_copies(0, True, sel.at[1], ext_span(0))
    down_copies = near_copies(1, False, sel.at[0], ext_span(1))
    near_start(True, up_copies)
    near_start(False, down_copies)

    @pl.when(jnp.logical_not(has_lower))
    def _():
        ext[:, own : own + margin] = jnp.zeros((vecs, margin), F32)

    @pl.when(jnp.logical_not(has_upper))
    def _():
        ext[:, own + margin :] = jnp.zeros((vecs, margin), F32)

    g_part[...] = dot_nt(vpad[...], vpad[...], HIGH)
    g_rows = nb // rows_n

    def g_span(which):
        return pl.ds(pl.multiple_of(which * g_rows, 8), g_rows)

    g_copies = row_copies(1, lambda peer: g_part.at[g_span(peer)], lambda k: g_rs.at[k - 1])

    for i in range(LOADS):
        loads[i].wait()

        @pl.loop(0, load_rows // 16)
        def _(j):
            span = pl.ds(pl.multiple_of(i * load_rows + j * 16, 16), 16)
            high, low = split_two(fac[span, :])
            fhi[span, :] = high
            flo[span, :] = low

    high, low = split_two(whole)
    stack[:vecs, :own] = high
    stack[vecs:, :own] = low
    step = 256

    def first_product(lo, hi, add):
        for j in range(0, share, step):
            both = dot_nt(stack[:, lo:hi], fhi[j : j + step, lo:hi])
            value = both[:vecs] + both[vecs:] + dot_nt(stack[:vecs, lo:hi], flo[j : j + step, lo:hi])
            acc[:, j : j + step] = acc[:, j : j + step] + value if add else value

    first_product(0, own, False)
    landed(g_copies)
    g_mine = g_part[g_span(row), :]
    for k in range(1, rows_n):
        g_mine = g_mine + g_rs[k - 1]
    g_sub[sub] = g_mine
    g_across = sub_copies(0, g_sub)

    near_wait(True, up_copies)
    near_wait(False, down_copies)
    high, low = split_two(ext[:, own:])
    stack[:vecs, own:] = high
    stack[vecs:, own:] = low
    first_product(own, wide, True)
    mine_cols = pl.ds(pl.multiple_of(row * share, 128), share)
    inner = acc[...] + ext[:, mine_cols]
    part[...] = jnp.zeros((vecs, wide), F32)
    part[:, mine_cols] = inner

    high, low = split_two(inner)
    both_in = jnp.concatenate([high, low], axis=0)

    def second_product(lo):
        both = dot_nn(both_in, fhi[:, lo : lo + slab])
        value = both[:vecs] + both[vecs:] + dot_nn(high, flo[:, lo : lo + slab])
        part[:, lo : lo + slab] = part[:, lo : lo + slab] + value

    for lo in range(own, wide, slab):
        second_product(lo)

    def margin_of(side, which):
        return part.at[:, pl.ds(pl.multiple_of(own + side * margin + which * quarter, 128), quarter)]

    mar0 = row_copies(3, lambda peer: margin_of(0, peer), lambda k: rs_mar.at[k - 1, 0])
    mar1 = row_copies(4, lambda peer: margin_of(1, peer), lambda k: rs_mar.at[k - 1, 1])
    for lo in range(0, own, slab):
        second_product(lo)

    def own_of(which):
        return part.at[:, pl.ds(pl.multiple_of(which * slab, 128), slab)]

    own_copies = row_copies(5, own_of, lambda k: rs_own.at[k - 1])
    landed(g_across)
    g_sum = g_sub[0]
    for k in range(1, subs):
        g_sum = g_sum + g_sub[k]
    g_full[g_span(row), :] = g_sum
    g_full[nb:, :] = jnp.zeros((g_full.shape[0] - nb, g_full.shape[1]), F32)
    g_gather = row_copies(
        2, lambda peer: g_full.at[g_span(row)], lambda k: g_full.at[g_span(row)]
    )
    landed(mar0)
    landed(mar1)
    for side in range(2):
        total = margin_of(side, row)[...]
        for k in range(1, rows_n):
            total = total + rs_mar[k - 1, side]
        back_q[side] = total

    def back_span(side):
        return back.at[:, pl.ds(pl.multiple_of(side * margin + row * quarter, 128), quarter)]

    back_down = near_copies(2, False, back_q.at[0], back_span(0))
    back_up = near_copies(3, True, back_q.at[1], back_span(1))
    near_start(False, back_down)
    near_start(True, back_up)

    @pl.when(jnp.logical_not(has_upper))
    def _():
        back[:, :margin] = jnp.zeros((vecs, margin), F32)

    @pl.when(jnp.logical_not(has_lower))
    def _():
        back[:, margin:] = jnp.zeros((vecs, margin), F32)

    my_rows = row * slab + lax.broadcasted_iota(jnp.int32, (slab, margin), 0)
    hot[:, :margin] = (my_rows == idx_ref[1:2, :]).astype(F32).astype(BF16)
    hot[:, margin:] = (my_rows == idx_ref[0:1, :]).astype(F32).astype(BF16)
    landed(own_copies)
    block_t = own_of(row)[...]
    for k in range(1, rows_n):
        block_t = block_t + rs_own[k - 1]
    near_wait(False, back_down)
    near_wait(True, back_up)
    added = dot_nt(jnp.concatenate(split_three(back[...]), axis=0), hot[...])
    block_t = block_t + (added[:vecs] + added[vecs : 2 * vecs] + added[2 * vecs :])

    def sum_all(value, slot, row_slot, by_row, by_sub):
        by_row[row] = value
        landed(row_copies(row_slot, lambda peer: by_row.at[row], lambda k: by_row.at[row]))
        total = by_row[0]
        for k in range(1, rows_n):
            total = total + by_row[k]
        by_sub[sub] = total
        landed(sub_copies(slot, by_sub))
        total = by_sub[0]
        for k in range(1, subs):
            total = total + by_sub[k]
        return total

    eighth = vecs // rows_n

    def vec_span(which):
        return pl.ds(pl.multiple_of(which * eighth, 8), eighth)

    f_part[...] = dot_nt(block_t, vpad[...], HIGH)
    landed(row_copies(6, lambda peer: f_part.at[vec_span(peer)], lambda k: f_row.at[k - 1]))
    first = f_part[vec_span(row), :]
    for k in range(1, rows_n):
        first = first + f_row[k - 1]
    f_sub[sub] = first
    landed(g_gather)
    landed(sub_copies(1, f_sub))
    first = f_sub[0]
    for k in range(1, subs):
        first = first + f_sub[k]
    second = first - dot_nn(first, g_full[...], HIGH)
    c_full[vec_span(row), :] = first + second
    landed(row_copies(8, lambda peer: c_full.at[vec_span(row)], lambda k: c_full.at[vec_span(row)]))
    coeffs = c_full[...]
    twice = block_t - dot_nn(coeffs, vpad[...], HIGH)
    gram = dot_nt(twice, twice, HIGH)
    fold = 128 // vecs
    tall = vecs // fold
    packed = jnp.concatenate([gram[i * tall : (i + 1) * tall] for i in range(fold)], axis=1)
    twice_ref[...] = twice
    coef_ref[...] = coeffs
    gram_ref[...] = sum_all(packed, 2, 7, c_row, c_sub) * (1.0 / total_rows)

    for copy in started:
        copy.wait_send()
    near_finish(True, up_copies)
    near_finish(False, down_copies)
    near_finish(False, back_down)
    near_finish(True, back_up)


def finish(packed_ref, twice_ref, coef_in, coef_ref, rfac_ref, q_ref):
    vecs = twice_ref.shape[0]
    packed = packed_ref[...]
    gram = jnp.concatenate(
        [packed[:, i : i + vecs] for i in range(0, packed.shape[1], vecs)], axis=0
    )
    coef_ref[...] = coef_in[:, : coef_ref.shape[1]]
    upper, inverse = factor_gram(gram, vecs)
    rfac_ref[...] = upper
    q_ref[:, 0, :] = dot_nn(inverse, twice_ref[...], HIGH)


def per_device(residual, factor, basis, send_rows):
    arrays = (residual, factor, basis, send_rows)
    subs = lax.axis_size("sub")
    rows_n = lax.axis_size("row")
    vecs, _, slab = residual.shape
    nb = basis.shape[0]
    _, share, wide = factor.shape
    margin = send_rows.shape[2]
    quarter = margin // rows_n
    pad = -(-nb // 128) * 128
    g_rows = nb // rows_n
    fold = 128 // vecs
    vmem = pl.BlockSpec(memory_space=pltpu.VMEM)
    hbm = pl.BlockSpec(memory_space=pltpu.HBM)
    coeffs, packed, twice = pl.pallas_call(
        functools.partial(kernel, subs, rows_n),
        out_shape=(
            jax.ShapeDtypeStruct((vecs, pad), F32),
            jax.ShapeDtypeStruct((vecs // fold, 128), F32),
            jax.ShapeDtypeStruct((vecs, slab), F32),
        ),
        in_specs=[hbm, hbm, hbm, hbm],
        out_specs=(vmem, vmem, vmem),
        scratch_shapes=[
            pltpu.VMEM((vecs, 1, slab), F32),
            pltpu.VMEM((nb, 1, slab), F32),
            pltpu.VMEM((2, margin), jnp.int32),
            pltpu.VMEM((share, wide), F32),
            pltpu.VMEM((share, wide), BF16),
            pltpu.VMEM((share, wide), BF16),
            pltpu.VMEM((vecs, wide), F32),
            pltpu.VMEM((2 * vecs, wide), BF16),
            pltpu.VMEM((2, vecs, quarter), F32),
            pltpu.VMEM((vecs, share), F32),
            pltpu.VMEM((vecs, wide), F32),
            pltpu.VMEM((rows_n - 1, vecs, slab), F32),
            pltpu.VMEM((rows_n - 1, 2, vecs, quarter), F32),
            pltpu.VMEM((2, vecs, quarter), F32),
            pltpu.VMEM((vecs, 2 * margin), F32),
            pltpu.VMEM((slab, 2 * margin), BF16),
            pltpu.VMEM((pad, slab), F32),
            pltpu.VMEM((pad, pad), F32),
            pltpu.VMEM((rows_n - 1, g_rows, pad), F32),
            pltpu.VMEM((subs, g_rows, pad), F32),
            pltpu.VMEM((pad, pad), F32),
            pltpu.VMEM((rows_n - 1, vecs // rows_n, pad), F32),
            pltpu.VMEM((subs, vecs // rows_n, pad), F32),
            pltpu.VMEM((rows_n, vecs // fold, 128), F32),
            pltpu.VMEM((subs, vecs // fold, 128), F32),
            pltpu.VMEM((vecs, pad), F32),
            pltpu.VMEM((vecs, pad), F32),
            pltpu.SemaphoreType.DMA((3,)),
            pltpu.SemaphoreType.DMA((LOADS,)),
            pltpu.SemaphoreType.DMA((9, rows_n - 1)),
            pltpu.SemaphoreType.DMA((9, rows_n - 1)),
            pltpu.SemaphoreType.DMA((4, rows_n)),
            pltpu.SemaphoreType.DMA((4, rows_n)),
            pltpu.SemaphoreType.DMA((3, subs - 1)),
            pltpu.SemaphoreType.DMA((3, subs - 1)),
        ],
        compiler_params=pltpu.CompilerParams(
            collective_id=0, has_side_effects=True, vmem_limit_bytes=40 * 1024 * 1024
        ),
        cost_estimate=pl.CostEstimate(
            flops=12 * vecs * share * wide, bytes_accessed=4 * share * wide, transcendentals=0
        ),
    )(*(pltpu.with_memory_space_constraint(array, pltpu.HBM) for array in arrays))
    coeffs, rfactor, block_q = pl.pallas_call(
        finish,
        out_shape=(
            jax.ShapeDtypeStruct((vecs, nb), F32),
            jax.ShapeDtypeStruct((vecs, vecs), F32),
            jax.ShapeDtypeStruct((vecs, 1, slab), F32),
        ),
        in_specs=[vmem, vmem, vmem],
        out_specs=(vmem, vmem, vmem),
    )(packed, twice, coeffs)
    return coeffs.T, rfactor, block_q


def solution(mesh):
    placed = (
        P(None, "sub", "row"),
        P("sub", "row", None),
        P(None, "sub", "row"),
        P("sub", None, None),
    )
    return jax.shard_map(
        per_device,
        mesh=mesh,
        in_specs=placed,
        out_specs=(P(), P(), P(None, "sub", "row")),
        check_vma=False,
    )
```

```python
import functools

import jax
import jax.numpy as jnp
from jax import lax
from jax.experimental import pallas as pl
from jax.experimental.pallas import tpu as pltpu
from jax.sharding import PartitionSpec as P

HIGH = lax.Precision.HIGHEST
MESH = pl.DeviceIdType.MESH
F32 = jnp.float32
BF16 = jnp.bfloat16
LOADS = 6


def dot_nt(left, right, precision=None):
    return lax.dot_general(
        left, right, (((1,), (1,)), ((), ())), precision=precision, preferred_element_type=F32
    )


def dot_nn(left, right, precision=None):
    return lax.dot_general(
        left, right, (((1,), (0,)), ((), ())), precision=precision, preferred_element_type=F32
    )


def split_two(value):
    high = value.astype(BF16)
    return high, (value - high.astype(F32)).astype(BF16)


def split_three(value):
    high = value.astype(BF16)
    rest = value - high.astype(F32)
    mid = rest.astype(BF16)
    return high, mid, (rest - mid.astype(F32)).astype(BF16)


def factor_gram(gram, vecs):
    eye = (
        lax.broadcasted_iota(jnp.int32, (vecs, vecs), 0)
        == lax.broadcasted_iota(jnp.int32, (vecs, vecs), 1)
    ).astype(F32)
    work = jnp.concatenate([gram, eye, jnp.zeros((vecs, 128 - 2 * vecs), F32)], axis=1)
    rows = lax.broadcasted_iota(jnp.int32, work.shape, 0)
    block = 8
    for start in range(0, vecs, block):
        spread = [
            jnp.broadcast_to(work[:, at : at + 1], work.shape) for at in range(start, start + block)
        ]
        for j in range(block):
            at = start + j
            if at == vecs - 1:
                break
            scale = 1.0 / spread[j][at : at + 1, :]
            multiplier = jnp.where(rows > at, spread[j] * scale, 0.0)
            for later in range(j + 1, block):
                spread[later] = spread[later] - multiplier * spread[later][at : at + 1, :]
            work = work - multiplier * work[at : at + 1, :]
    lanes = lax.broadcasted_iota(jnp.int32, work.shape, 1)
    pivots = jnp.sum(jnp.where(rows == lanes, work, 0.0), axis=1, keepdims=True)
    work = jnp.where(lanes >= rows, work, 0.0) * (1.0 / jnp.sqrt(pivots))
    return work[:, :vecs], work[:, vecs : 2 * vecs]


def kernel(
    subs,
    rows_n,
    res_hbm,
    fac_hbm,
    bas_hbm,
    idx_hbm,
    coef_ref,
    gram_ref,
    twice_ref,
    res_ref,
    bas_ref,
    idx_ref,
    fac,
    fhi,
    flo,
    ext,
    stack,
    sel,
    acc,
    part,
    rs_own,
    rs_mar,
    back_q,
    back,
    hot,
    vpad,
    g_part,
    g_rs,
    g_sub,
    g_full,
    f_row,
    f_sub,
    c_row,
    c_sub,
    f_part,
    c_full,
    small_sem,
    load_sem,
    row_send,
    row_recv,
    near_send,
    near_recv,
    sub_send,
    sub_recv,
):
    sub = lax.axis_index("sub")
    row = lax.axis_index("row")
    vecs, _, slab = res_ref.shape
    share, wide = fac.shape
    nb = bas_ref.shape[0]
    margin = idx_ref.shape[1]
    own = slab * rows_n
    quarter = margin // rows_n
    total_rows = own * subs
    has_lower = sub > 0
    has_upper = sub < subs - 1
    started = []

    def row_peer(k):
        return lax.rem(row + k, rows_n)

    def sub_peer(k):
        return lax.rem(sub + k, subs)

    small = [
        pltpu.make_async_copy(source, target, small_sem.at[i])
        for i, (source, target) in enumerate(
            [(res_hbm, res_ref), (idx_hbm.at[0], idx_ref), (bas_hbm, bas_ref)]
        )
    ]
    for copy in small:
        copy.start()
    load_rows = share // LOADS
    loads = []
    for i in range(LOADS):
        span = pl.ds(i * load_rows, load_rows)
        loads.append(pltpu.make_async_copy(fac_hbm.at[0, span], fac.at[span], load_sem.at[i]))
        loads[-1].start()

    barrier = pltpu.get_barrier_semaphore()

    def greet(to_sub, to_row):
        pl.semaphore_signal(barrier, inc=1, device_id=(to_sub, to_row), device_id_type=MESH)

    for k in range(1, rows_n):
        greet(sub, row_peer(k))

    @pl.when(has_lower)
    def _():
        for k in range(1, rows_n):
            greet(sub - 1, row_peer(k))

    @pl.when(has_upper)
    def _():
        for k in range(1, rows_n):
            greet(sub + 1, row_peer(k))

    for k in range(1, subs):
        greet(sub_peer(k), row)
    near = has_lower.astype(jnp.int32) + has_upper.astype(jnp.int32)
    own_slab = ext.at[:, pl.ds(pl.multiple_of(row * slab, 128), slab)]
    small[0].wait()
    own_slab[...] = res_ref[:, 0, :]
    pl.semaphore_wait(barrier, (rows_n - 1) * (1 + near) + subs - 1)

    def row_copies(slot, source_of, target_of):
        copies = []
        for k in range(1, rows_n):
            peer = row_peer(k)
            copies.append(
                pltpu.make_async_remote_copy(
                    source_of(peer),
                    target_of(k),
                    row_send.at[slot, k - 1],
                    row_recv.at[slot, k - 1],
                    device_id=(sub, peer),
                    device_id_type=MESH,
                )
            )
            copies[-1].start()
        started.extend(copies)
        return copies

    def sub_copies(slot, ref):
        copies = []
        for k in range(1, subs):
            copies.append(
                pltpu.make_async_remote_copy(
                    ref.at[sub],
                    ref.at[sub],
                    sub_send.at[slot, k - 1],
                    sub_recv.at[slot, k - 1],
                    device_id=(sub_peer(k), row),
                    device_id_type=MESH,
                )
            )
            copies[-1].start()
        started.extend(copies)
        return copies

    def near_copies(slot, up, source, target):
        to_sub = sub + 1 if up else sub - 1
        return [
            pltpu.make_async_remote_copy(
                source,
                target,
                near_send.at[slot, k],
                near_recv.at[slot, k],
                device_id=(to_sub, row_peer(k)),
                device_id_type=MESH,
            )
            for k in range(rows_n)
        ]

    def near_start(up, copies):
        @pl.when(has_upper if up else has_lower)
        def _():
            for copy in copies:
                copy.start()

    def near_wait(up, copies):
        @pl.when(has_lower if up else has_upper)
        def _():
            for copy in copies:
                copy.wait_recv()

    def near_finish(up, copies):
        @pl.when(has_upper if up else has_lower)
        def _():
            for copy in copies:
                copy.wait_send()

    def landed(copies):
        for copy in copies:
            copy.wait_recv()

    slab_copies = row_copies(0, lambda peer: own_slab, lambda k: own_slab)
    small[1].wait()
    base = lax.broadcasted_iota(jnp.int32, (own, quarter), 0)
    picks = []
    for side in range(2):
        index = idx_ref[side : side + 1, pl.ds(pl.multiple_of(row * quarter, 128), quarter)]
        picks.append((base == index).astype(F32).astype(BF16))
    pick = jnp.concatenate(picks, axis=1)
    small[2].wait()
    vpad[:nb] = bas_ref[:, 0, :]
    vpad[nb:] = jnp.zeros((vpad.shape[0] - nb, slab), F32)
    landed(slab_copies)
    whole = ext[:, :own]
    pieces = jnp.concatenate(split_three(whole), axis=0)
    chosen = dot_nn(pieces, pick)
    chosen = chosen[:vecs] + chosen[vecs : 2 * vecs] + chosen[2 * vecs :]
    sel[0] = chosen[:, :quarter]
    sel[1] = chosen[:, quarter:]

    def ext_span(side):
        return ext.at[:, pl.ds(pl.multiple_of(own + side * margin + row * quarter, 128), quarter)]

    up_copies = near_copies(0, True, sel.at[1], ext_span(0))
    down_copies = near_copies(1, False, sel.at[0], ext_span(1))
    near_start(True, up_copies)
    near_start(False, down_copies)

    @pl.when(jnp.logical_not(has_lower))
    def _():
        ext[:, own : own + margin] = jnp.zeros((vecs, margin), F32)

    @pl.when(jnp.logical_not(has_upper))
    def _():
        ext[:, own + margin :] = jnp.zeros((vecs, margin), F32)

    g_part[...] = dot_nt(vpad[...], vpad[...], HIGH)
    g_rows = nb // rows_n

    def g_span(which):
        return pl.ds(pl.multiple_of(which * g_rows, 8), g_rows)

    g_copies = row_copies(1, lambda peer: g_part.at[g_span(peer)], lambda k: g_rs.at[k - 1])

    for i in range(LOADS):
        loads[i].wait()

        @pl.loop(0, load_rows // 16)
        def _(j):
            span = pl.ds(pl.multiple_of(i * load_rows + j * 16, 16), 16)
            high, low = split_two(fac[span, :])
            fhi[span, :] = high
            flo[span, :] = low

    high, low = split_two(whole)
    stack[:vecs, :own] = high
    stack[vecs:, :own] = low
    step = 256

    def first_product(lo, hi, add):
        for j in range(0, share, step):
            both = dot_nt(stack[:, lo:hi], fhi[j : j + step, lo:hi])
            value = both[:vecs] + both[vecs:] + dot_nt(stack[:vecs, lo:hi], flo[j : j + step, lo:hi])
            acc[:, j : j + step] = acc[:, j : j + step] + value if add else value

    first_product(0, own, False)
    landed(g_copies)
    g_mine = g_part[g_span(row), :]
    for k in range(1, rows_n):
        g_mine = g_mine + g_rs[k - 1]
    g_sub[sub] = g_mine
    g_across = sub_copies(0, g_sub)

    near_wait(True, up_copies)
    near_wait(False, down_copies)
    high, low = split_two(ext[:, own:])
    stack[:vecs, own:] = high
    stack[vecs:, own:] = low
    first_product(own, wide, True)
    mine_cols = pl.ds(pl.multiple_of(row * share, 128), share)
    inner = acc[...] + ext[:, mine_cols]
    part[...] = jnp.zeros((vecs, wide), F32)
    part[:, mine_cols] = inner

    high, low = split_two(inner)
    both_in = jnp.concatenate([high, low], axis=0)

    def second_product(lo):
        both = dot_nn(both_in, fhi[:, lo : lo + slab])
        value = both[:vecs] + both[vecs:] + dot_nn(high, flo[:, lo : lo + slab])
        part[:, lo : lo + slab] = part[:, lo : lo + slab] + value

    for lo in range(own, wide, slab):
        second_product(lo)

    def margin_of(side, which):
        return part.at[:, pl.ds(pl.multiple_of(own + side * margin + which * quarter, 128), quarter)]

    mar0 = row_copies(3, lambda peer: margin_of(0, peer), lambda k: rs_mar.at[k - 1, 0])
    mar1 = row_copies(4, lambda peer: margin_of(1, peer), lambda k: rs_mar.at[k - 1, 1])
    for lo in range(0, own, slab):
        second_product(lo)

    def own_of(which):
        return part.at[:, pl.ds(pl.multiple_of(which * slab, 128), slab)]

    own_copies = row_copies(5, own_of, lambda k: rs_own.at[k - 1])
    landed(g_across)
    g_sum = g_sub[0]
    for k in range(1, subs):
        g_sum = g_sum + g_sub[k]
    g_full[g_span(row), :] = g_sum
    g_full[nb:, :] = jnp.zeros((g_full.shape[0] - nb, g_full.shape[1]), F32)
    g_gather = row_copies(
        2, lambda peer: g_full.at[g_span(row)], lambda k: g_full.at[g_span(row)]
    )
    landed(mar0)
    landed(mar1)
    for side in range(2):
        total = margin_of(side, row)[...]
        for k in range(1, rows_n):
            total = total + rs_mar[k - 1, side]
        back_q[side] = total

    def back_span(side):
        return back.at[:, pl.ds(pl.multiple_of(side * margin + row * quarter, 128), quarter)]

    back_down = near_copies(2, False, back_q.at[0], back_span(0))
    back_up = near_copies(3, True, back_q.at[1], back_span(1))
    near_start(False, back_down)
    near_start(True, back_up)

    @pl.when(jnp.logical_not(has_upper))
    def _():
        back[:, :margin] = jnp.zeros((vecs, margin), F32)

    @pl.when(jnp.logical_not(has_lower))
    def _():
        back[:, margin:] = jnp.zeros((vecs, margin), F32)

    my_rows = row * slab + lax.broadcasted_iota(jnp.int32, (slab, margin), 0)
    hot[:, :margin] = (my_rows == idx_ref[1:2, :]).astype(F32).astype(BF16)
    hot[:, margin:] = (my_rows == idx_ref[0:1, :]).astype(F32).astype(BF16)
    landed(own_copies)
    block_t = own_of(row)[...]
    for k in range(1, rows_n):
        block_t = block_t + rs_own[k - 1]
    near_wait(False, back_down)
    near_wait(True, back_up)
    added = dot_nt(jnp.concatenate(split_three(back[...]), axis=0), hot[...])
    block_t = block_t + (added[:vecs] + added[vecs : 2 * vecs] + added[2 * vecs :])

    def sum_all(value, slot, row_slot, by_row, by_sub):
        by_row[row] = value
        landed(row_copies(row_slot, lambda peer: by_row.at[row], lambda k: by_row.at[row]))
        total = by_row[0]
        for k in range(1, rows_n):
            total = total + by_row[k]
        by_sub[sub] = total
        landed(sub_copies(slot, by_sub))
        total = by_sub[0]
        for k in range(1, subs):
            total = total + by_sub[k]
        return total

    eighth = vecs // rows_n

    def vec_span(which):
        return pl.ds(pl.multiple_of(which * eighth, 8), eighth)

    f_part[...] = dot_nt(block_t, vpad[...], HIGH)
    landed(row_copies(6, lambda peer: f_part.at[vec_span(peer)], lambda k: f_row.at[k - 1]))
    first = f_part[vec_span(row), :]
    for k in range(1, rows_n):
        first = first + f_row[k - 1]
    f_sub[sub] = first
    landed(g_gather)
    landed(sub_copies(1, f_sub))
    first = f_sub[0]
    for k in range(1, subs):
        first = first + f_sub[k]
    second = first - dot_nn(first, g_full[...], HIGH)
    c_full[vec_span(row), :] = first + second
    landed(row_copies(8, lambda peer: c_full.at[vec_span(row)], lambda k: c_full.at[vec_span(row)]))
    coeffs = c_full[...]
    twice = block_t - dot_nn(coeffs, vpad[...], HIGH)
    gram = dot_nt(twice, twice, HIGH)
    fold = 128 // vecs
    tall = vecs // fold
    packed = jnp.concatenate([gram[i * tall : (i + 1) * tall] for i in range(fold)], axis=1)
    twice_ref[...] = twice
    coef_ref[...] = coeffs
    gram_ref[...] = sum_all(packed, 2, 7, c_row, c_sub) * (1.0 / total_rows)

    for copy in started:
        copy.wait_send()
    near_finish(True, up_copies)
    near_finish(False, down_copies)
    near_finish(False, back_down)
    near_finish(True, back_up)


def finish(packed_ref, twice_ref, coef_in, coef_ref, rfac_ref, q_ref):
    vecs = twice_ref.shape[0]
    packed = packed_ref[...]
    gram = jnp.concatenate(
        [packed[:, i : i + vecs] for i in range(0, packed.shape[1], vecs)], axis=0
    )
    coef_ref[...] = coef_in[:, : coef_ref.shape[1]]
    upper, inverse = factor_gram(gram, vecs)
    rfac_ref[...] = upper
    q_ref[:, 0, :] = dot_nn(inverse, twice_ref[...], HIGH)


def per_device(residual, factor, basis, send_rows):
    arrays = (residual, factor, basis, send_rows)
    subs = lax.axis_size("sub")
    rows_n = lax.axis_size("row")
    vecs, _, slab = residual.shape
    nb = basis.shape[0]
    _, share, wide = factor.shape
    margin = send_rows.shape[2]
    quarter = margin // rows_n
    pad = -(-nb // 128) * 128
    g_rows = nb // rows_n
    fold = 128 // vecs
    vmem = pl.BlockSpec(memory_space=pltpu.VMEM)
    hbm = pl.BlockSpec(memory_space=pltpu.HBM)
    coeffs, packed, twice = pl.pallas_call(
        functools.partial(kernel, subs, rows_n),
        out_shape=(
            jax.ShapeDtypeStruct((vecs, pad), F32),
            jax.ShapeDtypeStruct((vecs // fold, 128), F32),
            jax.ShapeDtypeStruct((vecs, slab), F32),
        ),
        in_specs=[hbm, hbm, hbm, hbm],
        out_specs=(vmem, vmem, vmem),
        scratch_shapes=[
            pltpu.VMEM((vecs, 1, slab), F32),
            pltpu.VMEM((nb, 1, slab), F32),
            pltpu.VMEM((2, margin), jnp.int32),
            pltpu.VMEM((share, wide), F32),
            pltpu.VMEM((share, wide), BF16),
            pltpu.VMEM((share, wide), BF16),
            pltpu.VMEM((vecs, wide), F32),
            pltpu.VMEM((2 * vecs, wide), BF16),
            pltpu.VMEM((2, vecs, quarter), F32),
            pltpu.VMEM((vecs, share), F32),
            pltpu.VMEM((vecs, wide), F32),
            pltpu.VMEM((rows_n - 1, vecs, slab), F32),
            pltpu.VMEM((rows_n - 1, 2, vecs, quarter), F32),
            pltpu.VMEM((2, vecs, quarter), F32),
            pltpu.VMEM((vecs, 2 * margin), F32),
            pltpu.VMEM((slab, 2 * margin), BF16),
            pltpu.VMEM((pad, slab), F32),
            pltpu.VMEM((pad, pad), F32),
            pltpu.VMEM((rows_n - 1, g_rows, pad), F32),
            pltpu.VMEM((subs, g_rows, pad), F32),
            pltpu.VMEM((pad, pad), F32),
            pltpu.VMEM((rows_n - 1, vecs // rows_n, pad), F32),
            pltpu.VMEM((subs, vecs // rows_n, pad), F32),
            pltpu.VMEM((rows_n, vecs // fold, 128), F32),
            pltpu.VMEM((subs, vecs // fold, 128), F32),
            pltpu.VMEM((vecs, pad), F32),
            pltpu.VMEM((vecs, pad), F32),
            pltpu.SemaphoreType.DMA((3,)),
            pltpu.SemaphoreType.DMA((LOADS,)),
            pltpu.SemaphoreType.DMA((9, rows_n - 1)),
            pltpu.SemaphoreType.DMA((9, rows_n - 1)),
            pltpu.SemaphoreType.DMA((4, rows_n)),
            pltpu.SemaphoreType.DMA((4, rows_n)),
            pltpu.SemaphoreType.DMA((3, subs - 1)),
            pltpu.SemaphoreType.DMA((3, subs - 1)),
        ],
        compiler_params=pltpu.CompilerParams(
            collective_id=0, has_side_effects=True, vmem_limit_bytes=40 * 1024 * 1024
        ),
        cost_estimate=pl.CostEstimate(
            flops=12 * vecs * share * wide, bytes_accessed=4 * share * wide, transcendentals=0
        ),
    )(*(pltpu.with_memory_space_constraint(array, pltpu.HBM) for array in arrays))
    coeffs, rfactor, block_q = pl.pallas_call(
        finish,
        out_shape=(
            jax.ShapeDtypeStruct((vecs, nb), F32),
            jax.ShapeDtypeStruct((vecs, vecs), F32),
            jax.ShapeDtypeStruct((vecs, 1, slab), F32),
        ),
        in_specs=[vmem, vmem, vmem],
        out_specs=(vmem, vmem, vmem),
        compiler_params=pltpu.CompilerParams(vmem_limit_bytes=8 * 1024 * 1024),
    )(packed, twice, coeffs)
    return coeffs.T, rfactor, block_q


def solution(mesh):
    placed = (
        P(None, "sub", "row"),
        P("sub", "row", None),
        P(None, "sub", "row"),
        P("sub", None, None),
    )
    return jax.shard_map(
        per_device,
        mesh=mesh,
        in_specs=placed,
        out_specs=(P(), P(), P(None, "sub", "row")),
        check_vma=False,
    )
```

```python
import functools

import jax
import jax.numpy as jnp
from jax import lax
from jax.experimental import pallas as pl
from jax.experimental.pallas import tpu as pltpu
from jax.sharding import PartitionSpec as P

HIGH = lax.Precision.HIGHEST
MESH = pl.DeviceIdType.MESH
F32 = jnp.float32
BF16 = jnp.bfloat16
LOADS = 6


def dot_nt(left, right, precision=None):
    return lax.dot_general(
        left, right, (((1,), (1,)), ((), ())), precision=precision, preferred_element_type=F32
    )


def dot_nn(left, right, precision=None):
    return lax.dot_general(
        left, right, (((1,), (0,)), ((), ())), precision=precision, preferred_element_type=F32
    )


def split_two(value):
    high = value.astype(BF16)
    return high, (value - high.astype(F32)).astype(BF16)


def split_three(value):
    high = value.astype(BF16)
    rest = value - high.astype(F32)
    mid = rest.astype(BF16)
    return high, mid, (rest - mid.astype(F32)).astype(BF16)


def factor_gram(gram, vecs):
    eye = (
        lax.broadcasted_iota(jnp.int32, (vecs, vecs), 0)
        == lax.broadcasted_iota(jnp.int32, (vecs, vecs), 1)
    ).astype(F32)
    work = jnp.concatenate([gram, eye, jnp.zeros((vecs, 128 - 2 * vecs), F32)], axis=1)
    rows = lax.broadcasted_iota(jnp.int32, work.shape, 0)
    block = 8
    for start in range(0, vecs, block):
        spread = [
            jnp.broadcast_to(work[:, at : at + 1], work.shape) for at in range(start, start + block)
        ]
        for j in range(block):
            at = start + j
            if at == vecs - 1:
                break
            scale = 1.0 / spread[j][at : at + 1, :]
            multiplier = jnp.where(rows > at, spread[j] * scale, 0.0)
            for later in range(j + 1, block):
                spread[later] = spread[later] - multiplier * spread[later][at : at + 1, :]
            work = work - multiplier * work[at : at + 1, :]
    lanes = lax.broadcasted_iota(jnp.int32, work.shape, 1)
    pivots = jnp.sum(jnp.where(rows == lanes, work, 0.0), axis=1, keepdims=True)
    work = jnp.where(lanes >= rows, work, 0.0) * (1.0 / jnp.sqrt(pivots))
    return work[:, :vecs], work[:, vecs : 2 * vecs]


def kernel(
    subs,
    rows_n,
    res_hbm,
    fac_hbm,
    bas_hbm,
    idx_hbm,
    coef_ref,
    gram_ref,
    twice_ref,
    res_ref,
    bas_ref,
    idx_ref,
    fac,
    fhi,
    flo,
    ext,
    stack,
    sel,
    acc,
    part,
    rs_own,
    rs_mar,
    back_q,
    back,
    hot,
    vpad,
    g_part,
    g_rs,
    g_sub,
    g_full,
    f_row,
    f_sub,
    c_row,
    c_sub,
    f_part,
    c_full,
    v_part,
    v_rs,
    v_quarter,
    v_mar,
    small_sem,
    load_sem,
    row_send,
    row_recv,
    near_send,
    near_recv,
    sub_send,
    sub_recv,
):
    sub = lax.axis_index("sub")
    row = lax.axis_index("row")
    vecs, _, slab = res_ref.shape
    share, wide = fac.shape
    nb = bas_ref.shape[0]
    margin = idx_ref.shape[1]
    own = slab * rows_n
    quarter = margin // rows_n
    total_rows = own * subs
    has_lower = sub > 0
    has_upper = sub < subs - 1
    started = []

    def row_peer(k):
        return lax.rem(row + k, rows_n)

    def sub_peer(k):
        return lax.rem(sub + k, subs)

    small = [
        pltpu.make_async_copy(source, target, small_sem.at[i])
        for i, (source, target) in enumerate(
            [(res_hbm, res_ref), (idx_hbm.at[0], idx_ref), (bas_hbm, bas_ref)]
        )
    ]
    for copy in small:
        copy.start()
    load_rows = share // LOADS
    loads = []
    for i in range(LOADS):
        span = pl.ds(i * load_rows, load_rows)
        loads.append(pltpu.make_async_copy(fac_hbm.at[0, span], fac.at[span], load_sem.at[i]))
        loads[-1].start()

    barrier = pltpu.get_barrier_semaphore()

    def greet(to_sub, to_row):
        pl.semaphore_signal(barrier, inc=1, device_id=(to_sub, to_row), device_id_type=MESH)

    for k in range(1, rows_n):
        greet(sub, row_peer(k))

    @pl.when(has_lower)
    def _():
        for k in range(1, rows_n):
            greet(sub - 1, row_peer(k))

    @pl.when(has_upper)
    def _():
        for k in range(1, rows_n):
            greet(sub + 1, row_peer(k))

    for k in range(1, subs):
        greet(sub_peer(k), row)
    near = has_lower.astype(jnp.int32) + has_upper.astype(jnp.int32)
    own_slab = ext.at[:, pl.ds(pl.multiple_of(row * slab, 128), slab)]
    small[0].wait()
    own_slab[...] = res_ref[:, 0, :]
    pl.semaphore_wait(barrier, (rows_n - 1) * (1 + near) + subs - 1)

    def row_copies(slot, source_of, target_of):
        copies = []
        for k in range(1, rows_n):
            peer = row_peer(k)
            copies.append(
                pltpu.make_async_remote_copy(
                    source_of(peer),
                    target_of(k),
                    row_send.at[slot, k - 1],
                    row_recv.at[slot, k - 1],
                    device_id=(sub, peer),
                    device_id_type=MESH,
                )
            )
            copies[-1].start()
        started.extend(copies)
        return copies

    def sub_copies(slot, ref):
        copies = []
        for k in range(1, subs):
            copies.append(
                pltpu.make_async_remote_copy(
                    ref.at[sub],
                    ref.at[sub],
                    sub_send.at[slot, k - 1],
                    sub_recv.at[slot, k - 1],
                    device_id=(sub_peer(k), row),
                    device_id_type=MESH,
                )
            )
            copies[-1].start()
        started.extend(copies)
        return copies

    def near_copies(slot, up, source, target, count=rows_n):
        to_sub = sub + 1 if up else sub - 1
        return [
            pltpu.make_async_remote_copy(
                source,
                target,
                near_send.at[slot, k],
                near_recv.at[slot, k],
                device_id=(to_sub, row_peer(k)),
                device_id_type=MESH,
            )
            for k in range(count)
        ]

    def near_start(up, copies):
        @pl.when(has_upper if up else has_lower)
        def _():
            for copy in copies:
                copy.start()

    def near_wait(up, copies):
        @pl.when(has_lower if up else has_upper)
        def _():
            for copy in copies:
                copy.wait_recv()

    def near_finish(up, copies):
        @pl.when(has_upper if up else has_lower)
        def _():
            for copy in copies:
                copy.wait_send()

    def landed(copies):
        for copy in copies:
            copy.wait_recv()

    slab_copies = row_copies(0, lambda peer: own_slab, lambda k: own_slab)
    small[1].wait()
    base = lax.broadcasted_iota(jnp.int32, (own, quarter), 0)
    picks = []
    for side in range(2):
        index = idx_ref[side : side + 1, pl.ds(pl.multiple_of(row * quarter, 128), quarter)]
        picks.append((base == index).astype(F32).astype(BF16))
    pick = jnp.concatenate(picks, axis=1)
    small[2].wait()
    vpad[:nb] = bas_ref[:, 0, :]
    vpad[nb:] = jnp.zeros((vpad.shape[0] - nb, slab), F32)
    my_rows = row * slab + lax.broadcasted_iota(jnp.int32, (slab, margin), 0)
    hot[:, :margin] = (my_rows == idx_ref[1:2, :]).astype(F32).astype(BF16)
    hot[:, margin:] = (my_rows == idx_ref[0:1, :]).astype(F32).astype(BF16)
    g_part[...] = dot_nt(vpad[...], vpad[...], HIGH)
    picked = dot_nn(jnp.concatenate(split_three(vpad[:nb]), axis=0), hot[...])
    picked = picked[:nb] + picked[nb : 2 * nb] + picked[2 * nb :]
    for which in range(rows_n):
        for side in range(2):
            at = side * margin + which * quarter
            v_part[which, side] = picked[:, at : at + quarter]
    landed(slab_copies)
    whole = ext[:, :own]
    pieces = jnp.concatenate(split_three(whole), axis=0)
    chosen = dot_nn(pieces, pick)
    chosen = chosen[:vecs] + chosen[vecs : 2 * vecs] + chosen[2 * vecs :]
    sel[0] = chosen[:, :quarter]
    sel[1] = chosen[:, quarter:]

    def ext_span(side):
        return ext.at[:, pl.ds(pl.multiple_of(own + side * margin + row * quarter, 128), quarter)]

    up_copies = near_copies(0, True, sel.at[1], ext_span(0))
    down_copies = near_copies(1, False, sel.at[0], ext_span(1))
    near_start(True, up_copies)
    near_start(False, down_copies)

    @pl.when(jnp.logical_not(has_lower))
    def _():
        ext[:, own : own + margin] = jnp.zeros((vecs, margin), F32)

    @pl.when(jnp.logical_not(has_upper))
    def _():
        ext[:, own + margin :] = jnp.zeros((vecs, margin), F32)

    g_rows = nb // rows_n

    def g_span(which):
        return pl.ds(pl.multiple_of(which * g_rows, 8), g_rows)

    v_copies = row_copies(9, lambda peer: v_part.at[peer], lambda k: v_rs.at[k - 1])
    g_copies = row_copies(1, lambda peer: g_part.at[g_span(peer)], lambda k: g_rs.at[k - 1])

    for i in range(LOADS):
        loads[i].wait()

        @pl.loop(0, load_rows // 16)
        def _(j):
            span = pl.ds(pl.multiple_of(i * load_rows + j * 16, 16), 16)
            high, low = split_two(fac[span, :])
            fhi[span, :] = high
            flo[span, :] = low

    high, low = split_two(whole)
    stack[:vecs, :own] = high
    stack[vecs:, :own] = low
    step = 256

    def first_product(lo, hi, add):
        for j in range(0, share, step):
            both = dot_nt(stack[:, lo:hi], fhi[j : j + step, lo:hi])
            value = both[:vecs] + both[vecs:] + dot_nt(stack[:vecs, lo:hi], flo[j : j + step, lo:hi])
            acc[:, j : j + step] = acc[:, j : j + step] + value if add else value

    first_product(0, own, False)
    landed(g_copies)
    g_mine = g_part[g_span(row), :]
    for k in range(1, rows_n):
        g_mine = g_mine + g_rs[k - 1]
    g_sub[sub] = g_mine
    landed(v_copies)
    for side in range(2):
        total = v_part[row, side]
        for k in range(1, rows_n):
            total = total + v_rs[k - 1, side]
        v_quarter[side] = total
    v_up = near_copies(4, True, v_quarter.at[0], v_mar.at[0, :nb], 1)
    v_down = near_copies(5, False, v_quarter.at[1], v_mar.at[1, :nb], 1)
    near_start(True, v_up)
    near_start(False, v_down)
    for side in range(2):
        v_mar[side, nb:, :] = jnp.zeros((v_mar.shape[1] - nb, quarter), F32)

    @pl.when(jnp.logical_not(has_lower))
    def _():
        v_mar[0, :nb, :] = jnp.zeros((nb, quarter), F32)

    @pl.when(jnp.logical_not(has_upper))
    def _():
        v_mar[1, :nb, :] = jnp.zeros((nb, quarter), F32)

    g_across = sub_copies(0, g_sub)

    near_wait(True, up_copies)
    near_wait(False, down_copies)
    high, low = split_two(ext[:, own:])
    stack[:vecs, own:] = high
    stack[vecs:, own:] = low
    first_product(own, wide, True)
    mine_cols = pl.ds(pl.multiple_of(row * share, 128), share)
    inner = acc[...] + ext[:, mine_cols]
    part[...] = jnp.zeros((vecs, wide), F32)
    part[:, mine_cols] = inner

    high, low = split_two(inner)
    both_in = jnp.concatenate([high, low], axis=0)

    def second_product(lo):
        both = dot_nn(both_in, fhi[:, lo : lo + slab])
        value = both[:vecs] + both[vecs:] + dot_nn(high, flo[:, lo : lo + slab])
        part[:, lo : lo + slab] = part[:, lo : lo + slab] + value

    for lo in range(own, wide, slab):
        second_product(lo)

    def margin_of(side, which):
        return part.at[:, pl.ds(pl.multiple_of(own + side * margin + which * quarter, 128), quarter)]

    mar0 = row_copies(3, lambda peer: margin_of(0, peer), lambda k: rs_mar.at[k - 1, 0])
    mar1 = row_copies(4, lambda peer: margin_of(1, peer), lambda k: rs_mar.at[k - 1, 1])
    for lo in range(0, own, slab):
        second_product(lo)

    def own_of(which):
        return part.at[:, pl.ds(pl.multiple_of(which * slab, 128), slab)]

    own_copies = row_copies(5, own_of, lambda k: rs_own.at[k - 1])
    landed(g_across)
    g_sum = g_sub[0]
    for k in range(1, subs):
        g_sum = g_sum + g_sub[k]
    g_full[g_span(row), :] = g_sum
    g_full[nb:, :] = jnp.zeros((g_full.shape[0] - nb, g_full.shape[1]), F32)
    g_gather = row_copies(
        2, lambda peer: g_full.at[g_span(row)], lambda k: g_full.at[g_span(row)]
    )
    landed(mar0)
    landed(mar1)
    for side in range(2):
        total = margin_of(side, row)[...]
        for k in range(1, rows_n):
            total = total + rs_mar[k - 1, side]
        back_q[side] = total

    def back_span(side):
        return back.at[:, pl.ds(pl.multiple_of(side * margin + row * quarter, 128), quarter)]

    back_down = near_copies(2, False, back_q.at[0], back_span(0))
    back_up = near_copies(3, True, back_q.at[1], back_span(1))
    near_start(False, back_down)
    near_start(True, back_up)

    @pl.when(jnp.logical_not(has_upper))
    def _():
        back[:, :margin] = jnp.zeros((vecs, margin), F32)

    @pl.when(jnp.logical_not(has_lower))
    def _():
        back[:, margin:] = jnp.zeros((vecs, margin), F32)

    landed(own_copies)
    block_t = own_of(row)[...]
    for k in range(1, rows_n):
        block_t = block_t + rs_own[k - 1]
    def sum_all(value, slot, row_slot, by_row, by_sub):
        by_row[row] = value
        landed(row_copies(row_slot, lambda peer: by_row.at[row], lambda k: by_row.at[row]))
        total = by_row[0]
        for k in range(1, rows_n):
            total = total + by_row[k]
        by_sub[sub] = total
        landed(sub_copies(slot, by_sub))
        total = by_sub[0]
        for k in range(1, subs):
            total = total + by_sub[k]
        return total

    eighth = vecs // rows_n

    def vec_span(which):
        return pl.ds(pl.multiple_of(which * eighth, 8), eighth)

    near_wait(True, v_up)
    near_wait(False, v_down)
    f_part[...] = (
        dot_nt(block_t, vpad[...], HIGH)
        + dot_nt(back_q[0], v_mar[0], HIGH)
        + dot_nt(back_q[1], v_mar[1], HIGH)
    )
    landed(row_copies(6, lambda peer: f_part.at[vec_span(peer)], lambda k: f_row.at[k - 1]))
    first = f_part[vec_span(row), :]
    for k in range(1, rows_n):
        first = first + f_row[k - 1]
    f_sub[sub] = first
    f_across = sub_copies(1, f_sub)
    near_wait(False, back_down)
    near_wait(True, back_up)
    added = dot_nt(jnp.concatenate(split_three(back[...]), axis=0), hot[...])
    block_t = block_t + (added[:vecs] + added[vecs : 2 * vecs] + added[2 * vecs :])
    landed(g_gather)
    landed(f_across)
    first = f_sub[0]
    for k in range(1, subs):
        first = first + f_sub[k]
    second = first - dot_nn(first, g_full[...], HIGH)
    c_full[vec_span(row), :] = first + second
    landed(row_copies(8, lambda peer: c_full.at[vec_span(row)], lambda k: c_full.at[vec_span(row)]))
    coeffs = c_full[...]
    twice = block_t - dot_nn(coeffs, vpad[...], HIGH)
    gram = dot_nt(twice, twice, HIGH)
    fold = 128 // vecs
    tall = vecs // fold
    packed = jnp.concatenate([gram[i * tall : (i + 1) * tall] for i in range(fold)], axis=1)
    twice_ref[...] = twice
    coef_ref[...] = coeffs
    gram_ref[...] = sum_all(packed, 2, 7, c_row, c_sub) * (1.0 / total_rows)

    for copy in started:
        copy.wait_send()
    near_finish(True, up_copies)
    near_finish(False, down_copies)
    near_finish(False, back_down)
    near_finish(True, back_up)
    near_finish(True, v_up)
    near_finish(False, v_down)


def finish(packed_ref, twice_ref, coef_in, coef_ref, rfac_ref, q_ref):
    vecs = twice_ref.shape[0]
    packed = packed_ref[...]
    gram = jnp.concatenate(
        [packed[:, i : i + vecs] for i in range(0, packed.shape[1], vecs)], axis=0
    )
    coef_ref[...] = coef_in[:, : coef_ref.shape[1]]
    upper, inverse = factor_gram(gram, vecs)
    rfac_ref[...] = upper
    q_ref[:, 0, :] = dot_nn(inverse, twice_ref[...], HIGH)


def per_device(residual, factor, basis, send_rows):
    arrays = (residual, factor, basis, send_rows)
    subs = lax.axis_size("sub")
    rows_n = lax.axis_size("row")
    vecs, _, slab = residual.shape
    nb = basis.shape[0]
    _, share, wide = factor.shape
    margin = send_rows.shape[2]
    quarter = margin // rows_n
    pad = -(-nb // 128) * 128
    g_rows = nb // rows_n
    fold = 128 // vecs
    vmem = pl.BlockSpec(memory_space=pltpu.VMEM)
    hbm = pl.BlockSpec(memory_space=pltpu.HBM)
    coeffs, packed, twice = pl.pallas_call(
        functools.partial(kernel, subs, rows_n),
        out_shape=(
            jax.ShapeDtypeStruct((vecs, pad), F32),
            jax.ShapeDtypeStruct((vecs // fold, 128), F32),
            jax.ShapeDtypeStruct((vecs, slab), F32),
        ),
        in_specs=[hbm, hbm, hbm, hbm],
        out_specs=(vmem, vmem, vmem),
        scratch_shapes=[
            pltpu.VMEM((vecs, 1, slab), F32),
            pltpu.VMEM((nb, 1, slab), F32),
            pltpu.VMEM((2, margin), jnp.int32),
            pltpu.VMEM((share, wide), F32),
            pltpu.VMEM((share, wide), BF16),
            pltpu.VMEM((share, wide), BF16),
            pltpu.VMEM((vecs, wide), F32),
            pltpu.VMEM((2 * vecs, wide), BF16),
            pltpu.VMEM((2, vecs, quarter), F32),
            pltpu.VMEM((vecs, share), F32),
            pltpu.VMEM((vecs, wide), F32),
            pltpu.VMEM((rows_n - 1, vecs, slab), F32),
            pltpu.VMEM((rows_n - 1, 2, vecs, quarter), F32),
            pltpu.VMEM((2, vecs, quarter), F32),
            pltpu.VMEM((vecs, 2 * margin), F32),
            pltpu.VMEM((slab, 2 * margin), BF16),
            pltpu.VMEM((pad, slab), F32),
            pltpu.VMEM((pad, pad), F32),
            pltpu.VMEM((rows_n - 1, g_rows, pad), F32),
            pltpu.VMEM((subs, g_rows, pad), F32),
            pltpu.VMEM((pad, pad), F32),
            pltpu.VMEM((rows_n - 1, vecs // rows_n, pad), F32),
            pltpu.VMEM((subs, vecs // rows_n, pad), F32),
            pltpu.VMEM((rows_n, vecs // fold, 128), F32),
            pltpu.VMEM((subs, vecs // fold, 128), F32),
            pltpu.VMEM((vecs, pad), F32),
            pltpu.VMEM((vecs, pad), F32),
            pltpu.VMEM((rows_n, 2, nb, quarter), F32),
            pltpu.VMEM((rows_n - 1, 2, nb, quarter), F32),
            pltpu.VMEM((2, nb, quarter), F32),
            pltpu.VMEM((2, pad, quarter), F32),
            pltpu.SemaphoreType.DMA((3,)),
            pltpu.SemaphoreType.DMA((LOADS,)),
            pltpu.SemaphoreType.DMA((10, rows_n - 1)),
            pltpu.SemaphoreType.DMA((10, rows_n - 1)),
            pltpu.SemaphoreType.DMA((6, rows_n)),
            pltpu.SemaphoreType.DMA((6, rows_n)),
            pltpu.SemaphoreType.DMA((3, subs - 1)),
            pltpu.SemaphoreType.DMA((3, subs - 1)),
        ],
        compiler_params=pltpu.CompilerParams(
            collective_id=0, has_side_effects=True, vmem_limit_bytes=40 * 1024 * 1024
        ),
        cost_estimate=pl.CostEstimate(
            flops=12 * vecs * share * wide, bytes_accessed=4 * share * wide, transcendentals=0
        ),
    )(*(pltpu.with_memory_space_constraint(array, pltpu.HBM) for array in arrays))
    coeffs, rfactor, block_q = pl.pallas_call(
        finish,
        out_shape=(
            jax.ShapeDtypeStruct((vecs, nb), F32),
            jax.ShapeDtypeStruct((vecs, vecs), F32),
            jax.ShapeDtypeStruct((vecs, 1, slab), F32),
        ),
        in_specs=[vmem, vmem, vmem],
        out_specs=(vmem, vmem, vmem),
        compiler_params=pltpu.CompilerParams(vmem_limit_bytes=8 * 1024 * 1024),
    )(packed, twice, coeffs)
    return coeffs.T, rfactor, block_q


def solution(mesh):
    placed = (
        P(None, "sub", "row"),
        P("sub", "row", None),
        P(None, "sub", "row"),
        P("sub", None, None),
    )
    return jax.shard_map(
        per_device,
        mesh=mesh,
        in_specs=placed,
        out_specs=(P(), P(), P(None, "sub", "row")),
        check_vma=False,
    )
```

```python
import functools

import jax
import jax.numpy as jnp
from jax import lax
from jax.experimental import pallas as pl
from jax.experimental.pallas import tpu as pltpu
from jax.sharding import PartitionSpec as P

HIGH = lax.Precision.HIGHEST
MESH = pl.DeviceIdType.MESH
F32 = jnp.float32
BF16 = jnp.bfloat16
LOADS = 6


def dot_nt(left, right, precision=None):
    return lax.dot_general(
        left, right, (((1,), (1,)), ((), ())), precision=precision, preferred_element_type=F32
    )


def dot_nn(left, right, precision=None):
    return lax.dot_general(
        left, right, (((1,), (0,)), ((), ())), precision=precision, preferred_element_type=F32
    )


def split_two(value):
    high = value.astype(BF16)
    return high, (value - high.astype(F32)).astype(BF16)


def split_three(value):
    high = value.astype(BF16)
    rest = value - high.astype(F32)
    mid = rest.astype(BF16)
    return high, mid, (rest - mid.astype(F32)).astype(BF16)


def factor_gram(gram, vecs):
    eye = (
        lax.broadcasted_iota(jnp.int32, (vecs, vecs), 0)
        == lax.broadcasted_iota(jnp.int32, (vecs, vecs), 1)
    ).astype(F32)
    work = jnp.concatenate([gram, eye, jnp.zeros((vecs, 128 - 2 * vecs), F32)], axis=1)
    rows = lax.broadcasted_iota(jnp.int32, work.shape, 0)
    block = 8
    for start in range(0, vecs, block):
        spread = [
            jnp.broadcast_to(work[:, at : at + 1], work.shape) for at in range(start, start + block)
        ]
        for j in range(block):
            at = start + j
            if at == vecs - 1:
                break
            scale = 1.0 / spread[j][at : at + 1, :]
            multiplier = jnp.where(rows > at, spread[j] * scale, 0.0)
            for later in range(j + 1, block):
                spread[later] = spread[later] - multiplier * spread[later][at : at + 1, :]
            work = work - multiplier * work[at : at + 1, :]
    lanes = lax.broadcasted_iota(jnp.int32, work.shape, 1)
    pivots = jnp.sum(jnp.where(rows == lanes, work, 0.0), axis=1, keepdims=True)
    work = jnp.where(lanes >= rows, work, 0.0) * (1.0 / jnp.sqrt(pivots))
    return work[:, :vecs], work[:, vecs : 2 * vecs]


def kernel(
    subs,
    rows_n,
    res_hbm,
    fac_hbm,
    bas_hbm,
    idx_hbm,
    coef_ref,
    gram_ref,
    twice_ref,
    res_ref,
    bas_ref,
    idx_ref,
    fac,
    fhi,
    flo,
    ext,
    stack,
    sel,
    acc,
    part,
    rs_own,
    rs_mar,
    back_q,
    back,
    hot,
    vpad,
    g_part,
    g_rs,
    g_sub,
    g_full,
    f_row,
    f_sub,
    c_row,
    c_sub,
    f_part,
    c_full,
    small_sem,
    load_sem,
    row_send,
    row_recv,
    near_send,
    near_recv,
    sub_send,
    sub_recv,
):
    sub = lax.axis_index("sub")
    row = lax.axis_index("row")
    vecs, _, slab = res_ref.shape
    share, wide = fac.shape
    nb = bas_ref.shape[0]
    margin = idx_ref.shape[1]
    own = slab * rows_n
    quarter = margin // rows_n
    total_rows = own * subs
    has_lower = sub > 0
    has_upper = sub < subs - 1
    started = []

    def row_peer(k):
        return lax.rem(row + k, rows_n)

    def sub_peer(k):
        return lax.rem(sub + k, subs)

    small = [
        pltpu.make_async_copy(source, target, small_sem.at[i])
        for i, (source, target) in enumerate(
            [(res_hbm, res_ref), (idx_hbm.at[0], idx_ref), (bas_hbm, bas_ref)]
        )
    ]
    for copy in small:
        copy.start()
    load_rows = share // LOADS
    loads = []
    for i in range(LOADS):
        span = pl.ds(i * load_rows, load_rows)
        loads.append(pltpu.make_async_copy(fac_hbm.at[0, span], fac.at[span], load_sem.at[i]))
        loads[-1].start()

    barrier = pltpu.get_barrier_semaphore()

    def greet(to_sub, to_row):
        pl.semaphore_signal(barrier, inc=1, device_id=(to_sub, to_row), device_id_type=MESH)

    for k in range(1, rows_n):
        greet(sub, row_peer(k))

    @pl.when(has_lower)
    def _():
        for k in range(1, rows_n):
            greet(sub - 1, row_peer(k))

    @pl.when(has_upper)
    def _():
        for k in range(1, rows_n):
            greet(sub + 1, row_peer(k))

    for k in range(1, subs):
        greet(sub_peer(k), row)
    near = has_lower.astype(jnp.int32) + has_upper.astype(jnp.int32)
    own_slab = ext.at[:, pl.ds(pl.multiple_of(row * slab, 128), slab)]
    small[0].wait()
    own_slab[...] = res_ref[:, 0, :]
    pl.semaphore_wait(barrier, (rows_n - 1) * (1 + near) + subs - 1)

    def row_copies(slot, source_of, target_of):
        copies = []
        for k in range(1, rows_n):
            peer = row_peer(k)
            copies.append(
                pltpu.make_async_remote_copy(
                    source_of(peer),
                    target_of(k),
                    row_send.at[slot, k - 1],
                    row_recv.at[slot, k - 1],
                    device_id=(sub, peer),
                    device_id_type=MESH,
                )
            )
            copies[-1].start()
        started.extend(copies)
        return copies

    def sub_copies(slot, ref):
        copies = []
        for k in range(1, subs):
            copies.append(
                pltpu.make_async_remote_copy(
                    ref.at[sub],
                    ref.at[sub],
                    sub_send.at[slot, k - 1],
                    sub_recv.at[slot, k - 1],
                    device_id=(sub_peer(k), row),
                    device_id_type=MESH,
                )
            )
            copies[-1].start()
        started.extend(copies)
        return copies

    def near_copies(slot, up, source, target):
        to_sub = sub + 1 if up else sub - 1
        return [
            pltpu.make_async_remote_copy(
                source,
                target,
                near_send.at[slot, k],
                near_recv.at[slot, k],
                device_id=(to_sub, row_peer(k)),
                device_id_type=MESH,
            )
            for k in range(rows_n)
        ]

    def near_start(up, copies):
        @pl.when(has_upper if up else has_lower)
        def _():
            for copy in copies:
                copy.start()

    def near_wait(up, copies):
        @pl.when(has_lower if up else has_upper)
        def _():
            for copy in copies:
                copy.wait_recv()

    def near_finish(up, copies):
        @pl.when(has_upper if up else has_lower)
        def _():
            for copy in copies:
                copy.wait_send()

    def landed(copies):
        for copy in copies:
            copy.wait_recv()

    slab_copies = row_copies(0, lambda peer: own_slab, lambda k: own_slab)
    small[1].wait()
    base = lax.broadcasted_iota(jnp.int32, (own, quarter), 0)
    picks = []
    for side in range(2):
        index = idx_ref[side : side + 1, pl.ds(pl.multiple_of(row * quarter, 128), quarter)]
        picks.append((base == index).astype(F32).astype(BF16))
    pick = jnp.concatenate(picks, axis=1)
    small[2].wait()
    vpad[:nb] = bas_ref[:, 0, :]
    vpad[nb:] = jnp.zeros((vpad.shape[0] - nb, slab), F32)
    g_part[...] = dot_nt(vpad[...], vpad[...], HIGH)
    def split_loads(first, last):
        for i in range(first, last):
            loads[i].wait()

            @pl.loop(0, load_rows // 16)
            def _(j):
                span = pl.ds(pl.multiple_of(i * load_rows + j * 16, 16), 16)
                high, low = split_two(fac[span, :])
                fhi[span, :] = high
                flo[span, :] = low

    split_loads(0, LOADS // 2)
    landed(slab_copies)
    whole = ext[:, :own]
    pieces = jnp.concatenate(split_three(whole), axis=0)
    chosen = dot_nn(pieces, pick)
    chosen = chosen[:vecs] + chosen[vecs : 2 * vecs] + chosen[2 * vecs :]
    sel[0] = chosen[:, :quarter]
    sel[1] = chosen[:, quarter:]

    def ext_span(side):
        return ext.at[:, pl.ds(pl.multiple_of(own + side * margin + row * quarter, 128), quarter)]

    up_copies = near_copies(0, True, sel.at[1], ext_span(0))
    down_copies = near_copies(1, False, sel.at[0], ext_span(1))
    near_start(True, up_copies)
    near_start(False, down_copies)

    @pl.when(jnp.logical_not(has_lower))
    def _():
        ext[:, own : own + margin] = jnp.zeros((vecs, margin), F32)

    @pl.when(jnp.logical_not(has_upper))
    def _():
        ext[:, own + margin :] = jnp.zeros((vecs, margin), F32)

    g_rows = nb // rows_n

    def g_span(which):
        return pl.ds(pl.multiple_of(which * g_rows, 8), g_rows)

    g_copies = row_copies(1, lambda peer: g_part.at[g_span(peer)], lambda k: g_rs.at[k - 1])

    split_loads(LOADS // 2, LOADS)

    high, low = split_two(whole)
    stack[:vecs, :own] = high
    stack[vecs:, :own] = low
    step = 256

    def first_product(lo, hi, add):
        for j in range(0, share, step):
            both = dot_nt(stack[:, lo:hi], fhi[j : j + step, lo:hi])
            value = both[:vecs] + both[vecs:] + dot_nt(stack[:vecs, lo:hi], flo[j : j + step, lo:hi])
            acc[:, j : j + step] = acc[:, j : j + step] + value if add else value

    first_product(0, own, False)
    landed(g_copies)
    g_mine = g_part[g_span(row), :]
    for k in range(1, rows_n):
        g_mine = g_mine + g_rs[k - 1]
    g_sub[sub] = g_mine
    g_across = sub_copies(0, g_sub)

    near_wait(True, up_copies)
    near_wait(False, down_copies)
    high, low = split_two(ext[:, own:])
    stack[:vecs, own:] = high
    stack[vecs:, own:] = low
    first_product(own, wide, True)
    mine_cols = pl.ds(pl.multiple_of(row * share, 128), share)
    inner = acc[...] + ext[:, mine_cols]
    part[...] = jnp.zeros((vecs, wide), F32)
    part[:, mine_cols] = inner

    high, low = split_two(inner)
    both_in = jnp.concatenate([high, low], axis=0)

    def second_product(lo):
        both = dot_nn(both_in, fhi[:, lo : lo + slab])
        value = both[:vecs] + both[vecs:] + dot_nn(high, flo[:, lo : lo + slab])
        part[:, lo : lo + slab] = part[:, lo : lo + slab] + value

    for lo in range(own, wide, slab):
        second_product(lo)

    def margin_of(side, which):
        return part.at[:, pl.ds(pl.multiple_of(own + side * margin + which * quarter, 128), quarter)]

    mar0 = row_copies(3, lambda peer: margin_of(0, peer), lambda k: rs_mar.at[k - 1, 0])
    mar1 = row_copies(4, lambda peer: margin_of(1, peer), lambda k: rs_mar.at[k - 1, 1])
    for lo in range(0, own, slab):
        second_product(lo)

    def own_of(which):
        return part.at[:, pl.ds(pl.multiple_of(which * slab, 128), slab)]

    own_copies = row_copies(5, own_of, lambda k: rs_own.at[k - 1])
    landed(g_across)
    g_sum = g_sub[0]
    for k in range(1, subs):
        g_sum = g_sum + g_sub[k]
    g_full[g_span(row), :] = g_sum
    g_full[nb:, :] = jnp.zeros((g_full.shape[0] - nb, g_full.shape[1]), F32)
    g_gather = row_copies(
        2, lambda peer: g_full.at[g_span(row)], lambda k: g_full.at[g_span(row)]
    )
    landed(mar0)
    landed(mar1)
    for side in range(2):
        total = margin_of(side, row)[...]
        for k in range(1, rows_n):
            total = total + rs_mar[k - 1, side]
        back_q[side] = total

    def back_span(side):
        return back.at[:, pl.ds(pl.multiple_of(side * margin + row * quarter, 128), quarter)]

    back_down = near_copies(2, False, back_q.at[0], back_span(0))
    back_up = near_copies(3, True, back_q.at[1], back_span(1))
    near_start(False, back_down)
    near_start(True, back_up)

    @pl.when(jnp.logical_not(has_upper))
    def _():
        back[:, :margin] = jnp.zeros((vecs, margin), F32)

    @pl.when(jnp.logical_not(has_lower))
    def _():
        back[:, margin:] = jnp.zeros((vecs, margin), F32)

    my_rows = row * slab + lax.broadcasted_iota(jnp.int32, (slab, margin), 0)
    hot[:, :margin] = (my_rows == idx_ref[1:2, :]).astype(F32).astype(BF16)
    hot[:, margin:] = (my_rows == idx_ref[0:1, :]).astype(F32).astype(BF16)
    landed(own_copies)
    block_t = own_of(row)[...]
    for k in range(1, rows_n):
        block_t = block_t + rs_own[k - 1]
    near_wait(False, back_down)
    near_wait(True, back_up)
    added = dot_nt(jnp.concatenate(split_three(back[...]), axis=0), hot[...])
    block_t = block_t + (added[:vecs] + added[vecs : 2 * vecs] + added[2 * vecs :])

    def sum_all(value, slot, row_slot, by_row, by_sub):
        by_row[row] = value
        landed(row_copies(row_slot, lambda peer: by_row.at[row], lambda k: by_row.at[row]))
        total = by_row[0]
        for k in range(1, rows_n):
            total = total + by_row[k]
        by_sub[sub] = total
        landed(sub_copies(slot, by_sub))
        total = by_sub[0]
        for k in range(1, subs):
            total = total + by_sub[k]
        return total

    eighth = vecs // rows_n

    def vec_span(which):
        return pl.ds(pl.multiple_of(which * eighth, 8), eighth)

    f_part[...] = dot_nt(block_t, vpad[...], HIGH)
    landed(row_copies(6, lambda peer: f_part.at[vec_span(peer)], lambda k: f_row.at[k - 1]))
    first = f_part[vec_span(row), :]
    for k in range(1, rows_n):
        first = first + f_row[k - 1]
    f_sub[sub] = first
    landed(g_gather)
    landed(sub_copies(1, f_sub))
    first = f_sub[0]
    for k in range(1, subs):
        first = first + f_sub[k]
    second = first - dot_nn(first, g_full[...], HIGH)
    c_full[vec_span(row), :] = first + second
    landed(row_copies(8, lambda peer: c_full.at[vec_span(row)], lambda k: c_full.at[vec_span(row)]))
    coeffs = c_full[...]
    twice = block_t - dot_nn(coeffs, vpad[...], HIGH)
    gram = dot_nt(twice, twice, HIGH)
    fold = 128 // vecs
    tall = vecs // fold
    packed = jnp.concatenate([gram[i * tall : (i + 1) * tall] for i in range(fold)], axis=1)
    twice_ref[...] = twice
    coef_ref[...] = coeffs
    gram_ref[...] = sum_all(packed, 2, 7, c_row, c_sub) * (1.0 / total_rows)

    for copy in started:
        copy.wait_send()
    near_finish(True, up_copies)
    near_finish(False, down_copies)
    near_finish(False, back_down)
    near_finish(True, back_up)


def finish(packed_ref, twice_ref, coef_in, coef_ref, rfac_ref, q_ref):
    vecs = twice_ref.shape[0]
    packed = packed_ref[...]
    gram = jnp.concatenate(
        [packed[:, i : i + vecs] for i in range(0, packed.shape[1], vecs)], axis=0
    )
    coef_ref[...] = coef_in[:, : coef_ref.shape[1]]
    upper, inverse = factor_gram(gram, vecs)
    rfac_ref[...] = upper
    q_ref[:, 0, :] = dot_nn(inverse, twice_ref[...], HIGH)


def per_device(residual, factor, basis, send_rows):
    arrays = (residual, factor, basis, send_rows)
    subs = lax.axis_size("sub")
    rows_n = lax.axis_size("row")
    vecs, _, slab = residual.shape
    nb = basis.shape[0]
    _, share, wide = factor.shape
    margin = send_rows.shape[2]
    quarter = margin // rows_n
    pad = -(-nb // 128) * 128
    g_rows = nb // rows_n
    fold = 128 // vecs
    vmem = pl.BlockSpec(memory_space=pltpu.VMEM)
    hbm = pl.BlockSpec(memory_space=pltpu.HBM)
    coeffs, packed, twice = pl.pallas_call(
        functools.partial(kernel, subs, rows_n),
        out_shape=(
            jax.ShapeDtypeStruct((vecs, pad), F32),
            jax.ShapeDtypeStruct((vecs // fold, 128), F32),
            jax.ShapeDtypeStruct((vecs, slab), F32),
        ),
        in_specs=[hbm, hbm, hbm, hbm],
        out_specs=(vmem, vmem, vmem),
        scratch_shapes=[
            pltpu.VMEM((vecs, 1, slab), F32),
            pltpu.VMEM((nb, 1, slab), F32),
            pltpu.VMEM((2, margin), jnp.int32),
            pltpu.VMEM((share, wide), F32),
            pltpu.VMEM((share, wide), BF16),
            pltpu.VMEM((share, wide), BF16),
            pltpu.VMEM((vecs, wide), F32),
            pltpu.VMEM((2 * vecs, wide), BF16),
            pltpu.VMEM((2, vecs, quarter), F32),
            pltpu.VMEM((vecs, share), F32),
            pltpu.VMEM((vecs, wide), F32),
            pltpu.VMEM((rows_n - 1, vecs, slab), F32),
            pltpu.VMEM((rows_n - 1, 2, vecs, quarter), F32),
            pltpu.VMEM((2, vecs, quarter), F32),
            pltpu.VMEM((vecs, 2 * margin), F32),
            pltpu.VMEM((slab, 2 * margin), BF16),
            pltpu.VMEM((pad, slab), F32),
            pltpu.VMEM((pad, pad), F32),
            pltpu.VMEM((rows_n - 1, g_rows, pad), F32),
            pltpu.VMEM((subs, g_rows, pad), F32),
            pltpu.VMEM((pad, pad), F32),
            pltpu.VMEM((rows_n - 1, vecs // rows_n, pad), F32),
            pltpu.VMEM((subs, vecs // rows_n, pad), F32),
            pltpu.VMEM((rows_n, vecs // fold, 128), F32),
            pltpu.VMEM((subs, vecs // fold, 128), F32),
            pltpu.VMEM((vecs, pad), F32),
            pltpu.VMEM((vecs, pad), F32),
            pltpu.SemaphoreType.DMA((3,)),
            pltpu.SemaphoreType.DMA((LOADS,)),
            pltpu.SemaphoreType.DMA((9, rows_n - 1)),
            pltpu.SemaphoreType.DMA((9, rows_n - 1)),
            pltpu.SemaphoreType.DMA((4, rows_n)),
            pltpu.SemaphoreType.DMA((4, rows_n)),
            pltpu.SemaphoreType.DMA((3, subs - 1)),
            pltpu.SemaphoreType.DMA((3, subs - 1)),
        ],
        compiler_params=pltpu.CompilerParams(
            collective_id=0, has_side_effects=True, vmem_limit_bytes=40 * 1024 * 1024
        ),
        cost_estimate=pl.CostEstimate(
            flops=12 * vecs * share * wide, bytes_accessed=4 * share * wide, transcendentals=0
        ),
    )(*(pltpu.with_memory_space_constraint(array, pltpu.HBM) for array in arrays))
    coeffs, rfactor, block_q = pl.pallas_call(
        finish,
        out_shape=(
            jax.ShapeDtypeStruct((vecs, nb), F32),
            jax.ShapeDtypeStruct((vecs, vecs), F32),
            jax.ShapeDtypeStruct((vecs, 1, slab), F32),
        ),
        in_specs=[vmem, vmem, vmem],
        out_specs=(vmem, vmem, vmem),
        compiler_params=pltpu.CompilerParams(vmem_limit_bytes=8 * 1024 * 1024),
    )(packed, twice, coeffs)
    return coeffs.T, rfactor, block_q


def solution(mesh):
    placed = (
        P(None, "sub", "row"),
        P("sub", "row", None),
        P(None, "sub", "row"),
        P("sub", None, None),
    )
    return jax.shard_map(
        per_device,
        mesh=mesh,
        in_specs=placed,
        out_specs=(P(), P(), P(None, "sub", "row")),
        check_vma=False,
    )
```
